32 devices in a mesh: replica: 2 (over y), tensor: 4 (over z), dp: 4 (over x, core).
Axes of the slice: x: 2, y: 2, z: 4, core: 2. Of those that a mesh axis runs over, the one named last changes fastest.
Arguments:
- residual: bfloat16 [2, 128, 8192], P(None, 'replica', 'dp'), parts along dimension 1
- queries: bfloat16 [2, 128, 8192], P(None, ('replica', 'dp'), 'tensor'), parts along dimension 1, may hold values from -6 to 6
- new_keys: bfloat16 [2, 128, 8, 128], P(None, ('replica', 'dp'), 'tensor'), parts along dimension 1, as said below
- new_values: bfloat16 [2, 128, 8, 128], P(None, ('replica', 'dp'), 'tensor'), parts along dimension 1, as said below
- key_cache: bfloat16 [128, 8, 1024, 128], P(('replica', 'dp'), 'tensor'), parts along dimension 0, as said below
- value_cache: bfloat16 [128, 8, 1024, 128], P(('replica', 'dp'), 'tensor'), parts along dimension 0, as said below
- lengths: int32 [128], P(('replica', 'dp')), parts along dimension 0, may hold values from 1 to 1022, as said below
- out_weight: bfloat16 [8192, 8192], P('tensor', 'dp'), may hold values from -0.5 to 0.5
- norm_gain: bfloat16 [8192], P('dp'), may hold values from 0.099609375 to 1.8984375
- gate_weight: bfloat16 [8192, 14336], P('dp', 'tensor'), may hold values from -0.0625 to 0.0625
- up_weight: bfloat16 [8192, 14336], P('dp', 'tensor'), may hold values from -0.0625 to 0.0625
- down_weight: bfloat16 [14336, 8192], P('tensor', 'dp'), may hold values from -0.125 to 0.125
Outputs:
- output: bfloat16 [2, 128, 8192], P(None, 'replica', 'dp'), parts along dimension 1
The draws below stay inside these ranges and needn't reach their ends.
There are 2 independent parts, one for each index of `replica`. The reference program is written for one: setup_inputs(seed, part) draws one part's arguments, and reference() takes and returns one part's arrays. A program takes and returns all parts, laid end to end along the dimension named above; an argument that names none is the same for every part. Nothing has to cross between parts.
Inputs may be any that keep to these rules, and one draw needn't show every extreme that they name: `lengths`: cached tokens of each sequence before the first step; some sequence has exactly 1022 in every draw. `key_cache`: head copies c and c2 with c // 1 == c2 // 1 hold equal entries. `value_cache`: head copies c and c2 with c // 1 == c2 // 1 hold equal entries. `new_keys`: head copies c and c2 with c // 1 == c2 // 1 hold equal entries. `new_values`: head copies c and c2 with c // 1 == c2 // 1 hold equal entries.
All inputs are finite; a program needn't handle non-finite values.
Results may differ from the reference program's by a relative error of at most 0.018.
Values may be sent and summed in bfloat16 or wider, within the bound.
No kernel may reach another device: no remote copies, remote signals or barrier semaphores. Data moves between devices by JAX's collectives and lax.ppermute only.
A program may use at most 192 MiB of HBM per device.

```python
import jax
import jax.numpy as jnp
from jax import lax

D = 8192
HEADS = 64
KVH = 8
HD = 128
FF = 14336
STEPS = 2
CTX = 1024
KVC = 8
SEQS = 64
N_TENSOR = 4


def copies(base, axis_index):
    return jnp.repeat(base, KVC // KVH, axis=axis_index)


def draw_residual(key, part):
    key = jax.random.fold_in(key, 11)
    main_key, row_key, jitter_key = jax.random.split(key, 3)
    shape = (STEPS, SEQS, D)
    jitter = jax.random.uniform(jitter_key, (D,), jnp.float32, -0.15, 0.15)
    columns = 10.0 ** (jnp.arange(D, dtype=jnp.float32) / D - 0.5 + jitter)
    rows = jnp.exp(jax.random.uniform(row_key, (STEPS, SEQS, 1), jnp.float32, -1.2, 1.1))
    base = jax.random.normal(main_key, shape, jnp.float32)
    return (base * rows * columns[None, None, :]).astype(jnp.bfloat16)


def draw_key_cache(key, part):
    key = jax.random.fold_in(key, 21)
    base_key = jax.random.fold_in(key, 0)
    shape = (SEQS, KVH, CTX, HD)
    base = jax.random.normal(base_key, shape, jnp.float32)
    return copies(base, 1).astype(jnp.bfloat16)


def draw_value_cache(key, part):
    key = jax.random.fold_in(key, 31)
    shape = (SEQS, KVH, CTX, HD)
    base = jax.random.normal(key, shape, jnp.float32)
    return copies(base, 1).astype(jnp.bfloat16)


def draw_new_keys(key, part):
    key = jax.random.fold_in(key, 51)
    shape = (STEPS, SEQS, KVH, HD)
    base = jax.random.normal(key, shape, jnp.float32)
    return copies(base, 2).astype(jnp.bfloat16)


def draw_new_values(key, part):
    key = jax.random.fold_in(key, 61)
    shape = (STEPS, SEQS, KVH, HD)
    base = jax.random.normal(key, shape, jnp.float32)
    return copies(base, 2).astype(jnp.bfloat16)


def draw_lengths(key, part):
    key = jax.random.fold_in(key, 41)
    first_key, second_key = jax.random.split(key, 2)
    drawn = jax.random.randint(first_key, (SEQS,), 1, CTX - STEPS + 1)
    chosen_spot = jax.random.randint(second_key, (), 0, SEQS)
    return jnp.where(jnp.arange(SEQS) == chosen_spot, CTX - STEPS, drawn).astype(jnp.int32)


def raised(array, own_key, source, target, blocks, factor):
    owner, partner = [(jnp.arange(array.shape[position]) // (array.shape[position] // blocks)).reshape([-1 if axis == position else 1 for axis in range(array.ndim)]) for position in (source, target)]
    chosen = jax.random.permutation(own_key, blocks)[partner]
    strong = (owner == chosen) | (owner == (partner + blocks // 2) % blocks)
    return jnp.where(strong, factor * array, array)


def shard_levels(rng, extent, cuts, smallest, largest):
    gain = 1.0
    for dim, blocks in cuts:
        steps = jax.random.uniform(jax.random.fold_in(jax.random.fold_in(rng, 6), dim), (blocks,), jnp.float32, smallest / len(cuts), largest / len(cuts))
        gain = gain * jnp.repeat(jnp.exp(steps), extent[dim] // blocks).reshape((-1,) + (1,) * (len(extent) - 1 - dim))
    return gain


def normal_values(own_key, shape, scale, limit, cuts=(), kind=jnp.bfloat16):
    entries = jax.random.normal(own_key, shape, jnp.float32) * scale
    if len(cuts) > 0:
        entries = shard_levels(own_key, shape, cuts, -0.22, 0.18) * entries
    return jnp.clip(entries, min=-limit, max=limit).astype(kind)


def heavy_noise(own_key, extent, width, most, cuts, heavy, kind=jnp.bfloat16):
    array = width * jax.random.normal(own_key, extent, jnp.float32)
    if cuts:
        array = array * shard_levels(own_key, extent, cuts, -0.22, 0.18)
    return jnp.clip(raised(array, jax.random.fold_in(own_key, 3), *heavy), -most, most).astype(kind)


def setup_inputs(seed: int = 0, part: int = 0) -> dict:
    splits = jax.random.split(jax.random.key(seed), 13)
    part_keys = jax.random.split(jax.random.fold_in(splits[12], part), 13)
    return {
        "residual": draw_residual(jax.random.fold_in(jax.random.fold_in(splits[12], part), 71), part),
        "queries": normal_values(part_keys[1], (STEPS, SEQS, HEADS * HD), 1.0, 6.0, ((1, 4), (2, 4))),
        "new_keys": draw_new_keys(jax.random.fold_in(jax.random.fold_in(splits[12], part), 71), part),
        "new_values": draw_new_values(jax.random.fold_in(jax.random.fold_in(splits[12], part), 71), part),
        "key_cache": draw_key_cache(jax.random.fold_in(jax.random.fold_in(splits[12], part), 71), part),
        "value_cache": draw_value_cache(jax.random.fold_in(jax.random.fold_in(splits[12], part), 71), part),
        "lengths": draw_lengths(jax.random.fold_in(jax.random.fold_in(splits[12], part), 71), part),
        "out_weight": normal_values(splits[7], (HEADS * HD, D), HD ** -0.5, 0.5, ((0, 4), (1, 4))),
        "norm_gain": jnp.clip(1.0 + 0.18 * jax.random.normal(splits[8], (D,), jnp.float32), 0.099609375, 1.8984375).astype(jnp.bfloat16),
        "gate_weight": normal_values(splits[9], (D, FF), D ** -0.5, 0.0625, ((0, 4), (1, 4))),
        "up_weight": normal_values(splits[10], (D, FF), D ** -0.5, 0.0625, ((0, 4), (1, 4))),
        "down_weight": heavy_noise(splits[11], (FF, D), (FF // 4) ** -0.5, 0.125, ((0, 4), (1, 4)), (0, 1, 4, 2.0)),
    }


def rounded(values):
    return lax.optimization_barrier(values.astype(jnp.bfloat16)).astype(jnp.float32)

def attend_one(pieces):
    seq_queries, fresh_keys, fresh_values, cached_keys, cached_values, seq_length = pieces
    group_size = HEADS // KVC
    scaling = HD ** (-0.5)
    grouped = seq_queries.reshape(STEPS, KVC, group_size, HD).astype(jnp.float32)
    cached = jnp.einsum('sgjd,gtd->sgjt', grouped, cached_keys.astype(jnp.float32)) * scaling
    alive_mask = jnp.arange(CTX) < seq_length
    cached = jnp.where(alive_mask[None, None, None, :], cached, -jnp.inf)
    recent = jnp.einsum('sgjd,rgd->sgjr', grouped, fresh_keys.astype(jnp.float32)) * scaling
    causal = jnp.arange(STEPS)[None, :] <= jnp.arange(STEPS)[:, None]
    recent = jnp.where(causal[:, None, None, :], recent, -jnp.inf)
    row_max = jnp.maximum(lax.optimization_barrier(jnp.max(cached, axis=-1)), lax.optimization_barrier(jnp.max(recent, axis=-1)))
    w_cached = jnp.exp(cached - row_max[..., None])
    w_recent = jnp.exp(recent - row_max[..., None])
    totals = lax.optimization_barrier(jnp.sum(w_cached, axis=-1)) + lax.optimization_barrier(jnp.sum(w_recent, axis=-1))
    blended = jnp.einsum('sgjt,gtd->sgjd', rounded(w_cached), cached_values.astype(jnp.float32))
    blended = blended + jnp.einsum('sgjr,rgd->sgjd', rounded(w_recent), fresh_values.astype(jnp.float32))
    return (blended / totals[..., None]).astype(jnp.bfloat16).reshape(STEPS, HEADS * HD)

def reference(residual, queries, new_keys, new_values, key_cache, value_cache, lengths, out_weight, norm_gain, gate_weight, up_weight, down_weight):
    per_seq = lax.map(attend_one, (jnp.swapaxes(queries, 0, 1), jnp.swapaxes(new_keys, 0, 1), jnp.swapaxes(new_values, 0, 1), key_cache, value_cache, lengths))
    heads_out = jnp.swapaxes(per_seq, 0, 1)
    row_count = STEPS * SEQS
    group_rows = heads_out.reshape(row_count, N_TENSOR, HEADS * HD // N_TENSOR).astype(jnp.float32)
    group_weights = out_weight.reshape(N_TENSOR, HEADS * HD // N_TENSOR, D).astype(jnp.float32)
    parts = jnp.einsum('rgk,gkd->grd', group_rows, group_weights)
    attn = lax.optimization_barrier(jnp.sum(rounded(parts), axis=0)).astype(jnp.bfloat16)
    mid = (residual.reshape(row_count, D).astype(jnp.float32) + attn.astype(jnp.float32)).astype(jnp.bfloat16)
    mid_wide = mid.astype(jnp.float32)
    inv_norm = lax.rsqrt(lax.optimization_barrier(jnp.mean(mid_wide * mid_wide, axis=1)) + 1e-05)
    normed = (mid_wide * norm_gain.astype(jnp.float32)[None, :]).astype(jnp.bfloat16)
    gate = inv_norm[:, None] * jnp.dot(normed, gate_weight, preferred_element_type=jnp.float32)
    up_proj = inv_norm[:, None] * jnp.dot(normed, up_weight, preferred_element_type=jnp.float32)
    hidden = (jax.nn.silu(gate) * up_proj).astype(jnp.bfloat16)
    ffn = jnp.dot(hidden, down_weight, preferred_element_type=jnp.float32)
    return (mid_wide + ffn).astype(jnp.bfloat16).reshape(STEPS, SEQS, D)
```

```python
import jax
import jax.numpy as jnp
from jax import lax
from jax.sharding import PartitionSpec as P

BF16 = jnp.bfloat16
F32 = jnp.float32


def add(a, b):
    return (a.astype(F32) + b.astype(F32)).astype(BF16)


def pick(halves, index):
    return lax.dynamic_index_in_dim(halves, index, 0, keepdims=False)


def in_order(mine, other, bit):
    first = jnp.where(bit == 0, mine, other)
    second = jnp.where(bit == 0, other, mine)
    return jnp.concatenate((first, second), axis=0)


def pairs(size, step):
    return [(i, i ^ step) for i in range(size)]


def sum_tensor(part, size):
    if size != 4:
        return lax.psum(part, "tensor")
    bit = lax.axis_index("tensor") % 2
    halves = part.reshape(2, part.shape[0] // 2, part.shape[1])
    got = lax.ppermute(pick(halves, 1 - bit), "tensor", pairs(4, 1))
    held = add(pick(halves, bit), got)
    held = add(held, lax.ppermute(held, "tensor", pairs(4, 2)))
    return in_order(held, lax.ppermute(held, "tensor", pairs(4, 1)), bit)


def levels(size):
    return [1 << k for k in range(size.bit_length() - 1)]


def sum_scatter_dp(part, size):
    me = lax.axis_index("dp")
    for step in levels(size):
        bit = (me // step) % 2
        halves = part.reshape(2, part.shape[0] // 2, part.shape[1])
        got = lax.ppermute(pick(halves, 1 - bit), "dp", pairs(size, step))
        part = add(pick(halves, bit), got)
    return part


def gather_dp(block, size):
    me = lax.axis_index("dp")
    for step in reversed(levels(size)):
        bit = (me // step) % 2
        block = in_order(block, lax.ppermute(block, "dp", pairs(size, step)), bit)
    return block


def sum_dp(value, size):
    for step in levels(size):
        value = value + lax.ppermute(value, "dp", pairs(size, step))
    return value


def body(
    residual,
    queries,
    new_keys,
    new_values,
    key_cache,
    value_cache,
    lengths,
    out_weight,
    norm_gain,
    gate_weight,
    up_weight,
    down_weight,
):
    dp = lax.axis_size("dp")
    tensor = lax.axis_size("tensor")
    steps_count, all_seqs, width_local = residual.shape
    local_seqs = queries.shape[1]
    local_copies = key_cache.shape[1]
    ctx_slots = key_cache.shape[2]
    head_size = key_cache.shape[3]
    local_heads = queries.shape[2] // head_size
    group_size = local_heads // local_copies
    scaling = head_size ** (-0.5)
    grouped = queries.reshape(steps_count, local_seqs, local_copies, group_size, head_size)
    cached = (
        jnp.einsum("sbgjd,bgtd->sbgjt", grouped, key_cache, preferred_element_type=jnp.float32)
        * scaling
    )
    alive_mask = jnp.arange(ctx_slots)[None, :] < lengths[:, None]
    cached = jnp.where(alive_mask[None, :, None, None, :], cached, -jnp.inf)
    recent = (
        jnp.einsum("sbgjd,rbgd->sbgjr", grouped, new_keys, preferred_element_type=jnp.float32)
        * scaling
    )
    causal = jnp.arange(steps_count)[None, :] <= jnp.arange(steps_count)[:, None]
    recent = jnp.where(causal[:, None, None, None, :], recent, -jnp.inf)
    row_max = jnp.maximum(jnp.max(cached, axis=-1), jnp.max(recent, axis=-1))
    w_cached = jnp.exp(cached - row_max[..., None])
    w_recent = jnp.exp(recent - row_max[..., None])
    totals = jnp.sum(w_cached, axis=-1) + jnp.sum(w_recent, axis=-1)
    blended = jnp.einsum(
        "sbgjt,bgtd->sbgjd",
        w_cached.astype(jnp.bfloat16),
        value_cache,
        preferred_element_type=jnp.float32,
    )
    blended = blended + jnp.einsum(
        "sbgjr,rbgd->sbgjd",
        w_recent.astype(jnp.bfloat16),
        new_values,
        preferred_element_type=jnp.float32,
    )
    heads_out = (
        (blended / totals[..., None])
        .astype(jnp.bfloat16)
        .reshape(steps_count, local_seqs, local_heads * head_size)
    )
    rows = gather_dp(heads_out.reshape(steps_count * local_seqs, -1), dp)
    row_count = steps_count * all_seqs
    order = [0] * dp
    for d in range(dp):
        place = 0
        for k, step in enumerate(levels(dp)):
            place = place * 2 + (d // step) % 2
        order[d] = place

    def to_rows(block):
        block = block.reshape(dp, steps_count, local_seqs, block.shape[-1])
        block = jnp.stack([block[order[d]] for d in range(dp)], axis=1)
        return block.reshape(row_count, block.shape[-1])

    rows = to_rows(rows)
    chunks = 2
    wide = width_local // chunks
    mids = []
    resid = residual.reshape(row_count, width_local)
    for c in range(chunks):
        cols = slice(c * wide, (c + 1) * wide)
        part = jnp.dot(rows, out_weight[:, cols], preferred_element_type=F32).astype(BF16)
        mids.append(add(resid[:, cols], sum_tensor(part, tensor)))
    mid = jnp.concatenate(mids, axis=1)
    mid_wide = mid.astype(F32)
    squares = sum_dp(jnp.sum(mid_wide * mid_wide, axis=1)[None, :], dp)
    full_width = width_local * dp
    inv_norm = lax.rsqrt(squares / full_width + 1e-05)
    normed = (mid_wide * norm_gain.astype(F32)[None, :]).astype(BF16)
    contract = (((0,), (1,)), ((), ()))
    gate_term = lax.dot_general(gate_weight, normed, contract, preferred_element_type=F32)
    up_term = lax.dot_general(up_weight, normed, contract, preferred_element_type=F32)
    both = jnp.concatenate((gate_term, up_term), axis=1).astype(BF16)
    both = sum_scatter_dp(both, dp).astype(F32)
    gate = both[:, :row_count] * inv_norm
    up_proj = both[:, row_count:] * inv_norm
    hidden = (jax.nn.silu(gate) * up_proj).astype(BF16)
    hidden = gather_dp(hidden, dp)
    outs = []
    for c in range(chunks):
        cols = slice(c * wide, (c + 1) * wide)
        part = lax.dot_general(
            hidden, down_weight[:, cols], (((0,), (0,)), ((), ())), preferred_element_type=F32
        ).astype(BF16)
        outs.append(add(mids[c], sum_tensor(part, tensor)))
    return jnp.concatenate(outs, axis=1).reshape(residual.shape)


def solution(mesh):
    in_specs = (
        P(None, "replica", "dp"),
        P(None, ("replica", "dp"), "tensor"),
        P(None, ("replica", "dp"), "tensor", None),
        P(None, ("replica", "dp"), "tensor", None),
        P(("replica", "dp"), "tensor", None, None),
        P(("replica", "dp"), "tensor", None, None),
        P(("replica", "dp")),
        P("tensor", "dp"),
        P("dp"),
        P("dp", "tensor"),
        P("dp", "tensor"),
        P("tensor", "dp"),
    )
    out_specs = P(None, "replica", "dp")
    return jax.shard_map(body, mesh=mesh, in_specs=in_specs, out_specs=out_specs, check_vma=False)
```

```python
import functools

import jax
import jax.numpy as jnp
from jax import lax
from jax.experimental import pallas as pl
from jax.experimental.pallas import tpu as pltpu
from jax.sharding import PartitionSpec as P

BF16 = jnp.bfloat16
F32 = jnp.float32
MIB = 1 << 20


def add(a, b):
    return (a.astype(F32) + b.astype(F32)).astype(BF16)


def sum_kernel(dtype, *refs):
    total = functools.reduce(jnp.add, [ref[...].astype(F32) for ref in refs[:-1]])
    refs[-1][...] = total.astype(dtype)


def total_of(*terms, dtype=BF16):
    vmem = pl.BlockSpec(memory_space=pltpu.VMEM)
    return pl.pallas_call(
        functools.partial(sum_kernel, dtype),
        in_specs=[vmem] * len(terms),
        out_specs=vmem,
        out_shape=jax.ShapeDtypeStruct(terms[0].shape, dtype),
        cost_estimate=cost(terms[0].size, 4 * terms[0].size),
        compiler_params=pltpu.CompilerParams(vmem_limit_bytes=2 * MIB),
    )(*terms)


def cost(flops, read):
    return pl.CostEstimate(flops=flops, bytes_accessed=read, transcendentals=0)


def attention_kernel(first, count, len_ref, q_hbm, k_hbm, v_hbm, nk_hbm, nv_hbm, w_hbm, *refs):
    o_ref, w_ref, q_ref, nk_ref, nv_ref, k_buf, v_buf, out_buf, sem, small_sem, w_sem = refs
    small = [
        pltpu.make_async_copy(src, dst, small_sem.at[k])
        for k, (src, dst) in enumerate(((q_hbm, q_ref), (nk_hbm, nk_ref), (nv_hbm, nv_ref)))
    ]
    for move in small:
        move.start()
    steps = q_ref.shape[0]
    _, copies, slots, head = k_hbm.shape
    group = q_ref.shape[2] // (copies * head)
    rows = steps * group
    part = 256
    parts = slots // part
    batch = 4
    scaling = head ** (-0.5)

    def moves(b, c):
        here = pl.ds(c * part, part)
        return (
            pltpu.make_async_copy(k_hbm.at[first + b, :, here], k_buf.at[b, :, here], sem.at[0, b]),
            pltpu.make_async_copy(v_hbm.at[first + b, :, here], v_buf.at[b, :, here], sem.at[1, b]),
        )

    def start(b, c):
        for move in moves(b, c):
            move.start()

    def clear(b, c):
        v_buf[b, :, c * part : (c + 1) * part] = jnp.zeros((copies, part, head), BF16)

    def wait(b, c):
        for move in moves(b, c):
            move.wait()

    for b in range(count):
        start(b, 0)
        for c in range(1, parts):
            live = len_ref[first + b] > c * part
            pl.when(live)(functools.partial(start, b, c))
            pl.when(jnp.logical_not(live))(functools.partial(clear, b, c))

    weight = pltpu.make_async_copy(w_hbm, w_ref, w_sem)
    weight.start()
    for move in small:
        move.wait()
    slot = lax.broadcasted_iota(jnp.int32, (rows, slots), 1)
    step = lax.broadcasted_iota(jnp.int32, (rows, 1), 0) // group
    for b0 in range(0, count, batch):
        work = [(b, g) for b in range(b0, min(b0 + batch, count)) for g in range(copies)]
        asked, recent = [], []
        for b, g in work:
            pick = [
                q_ref[s, first + b : first + b + 1, (g * group + j) * head : (g * group + j + 1) * head]
                for s in range(steps)
                for j in range(group)
            ]
            wide = jnp.concatenate([p.astype(F32) for p in pick], axis=0)
            asked.append(wide.astype(BF16))
            found = []
            for r in range(steps):
                key = nk_ref[r, first + b, g : g + 1, :].astype(F32)
                score = jnp.sum(wide * key, axis=1, keepdims=True) * scaling
                found.append(jnp.where(step >= r, score, -jnp.inf))
            recent.append(found)
        for b in range(b0, min(b0 + batch, count)):
            wait(b, 0)
            for c in range(1, parts):
                pl.when(len_ref[first + b] > c * part)(functools.partial(wait, b, c))
        scores = [
            lax.dot_general(q, k_buf[b, g], (((1,), (1,)), ((), ())), preferred_element_type=F32)
            for q, (b, g) in zip(asked, work)
        ]
        scores = [
            jnp.where(slot < len_ref[first + b], s * scaling, -jnp.inf)
            for s, (b, g) in zip(scores, work)
        ]
        tops = [
            functools.reduce(jnp.maximum, [jnp.max(s, axis=1, keepdims=True)] + found)
            for s, found in zip(scores, recent)
        ]
        weights = [jnp.exp(s - top) for s, top in zip(scores, tops)]
        fresh = [[jnp.exp(x - top) for x in found] for found, top in zip(recent, tops)]
        totals = [jnp.sum(w, axis=1, keepdims=True) + sum(f) for w, f in zip(weights, fresh)]
        blends = [
            jnp.dot(w.astype(BF16), v_buf[b, g], preferred_element_type=F32)
            for w, (b, g) in zip(weights, work)
        ]
        for (b, g), blend, f, total in zip(work, blends, fresh, totals):
            for r in range(steps):
                value = nv_ref[r, first + b, g : g + 1, :].astype(F32)
                blend = blend + f[r].astype(BF16).astype(F32) * value
            out = blend / total
            for s in range(steps):
                for j in range(group):
                    cols = slice((g * group + j) * head, (g * group + j + 1) * head)
                    at = s * count + b
                    out_buf[at : at + 1, cols] = out[s * group + j : s * group + j + 1, :]
    o_ref[...] = out_buf[...].astype(BF16)
    weight.wait()


def attention(queries, new_keys, new_values, key_cache, value_cache, lengths, weight):
    first, count = 0, queries.shape[1]
    steps, _, deep = queries.shape
    _, copies, slots, head = key_cache.shape
    vmem = pl.BlockSpec(memory_space=pltpu.VMEM)
    hbm = pl.BlockSpec(memory_space=pl.ANY)
    buffer = pltpu.VMEM((count, copies, slots, head), BF16)
    moved = [queries, key_cache, value_cache, new_keys, new_values, weight]
    moved = [pltpu.with_memory_space_constraint(x, pltpu.HBM) for x in moved]
    return pl.pallas_call(
        functools.partial(attention_kernel, first, count),
        in_specs=[pl.BlockSpec(memory_space=pltpu.SMEM)] + [hbm] * 6,
        out_specs=[vmem, vmem],
        out_shape=[
            jax.ShapeDtypeStruct((steps * count, deep), BF16),
            pltpu.VMEM(weight.shape, weight.dtype),
        ],
        scratch_shapes=[
            pltpu.VMEM(queries.shape, BF16),
            pltpu.VMEM(new_keys.shape, BF16),
            pltpu.VMEM(new_values.shape, BF16),
            buffer,
            buffer,
            pltpu.VMEM((steps * count, deep), F32),
            pltpu.SemaphoreType.DMA((2, count)),
            pltpu.SemaphoreType.DMA((3,)),
            pltpu.SemaphoreType.DMA(()),
        ],
        cost_estimate=cost(4 * steps * count * slots * deep, 4 * count * copies * slots * head),
        compiler_params=pltpu.CompilerParams(vmem_limit_bytes=40 * MIB),
    )(lengths, *moved)


def fetch_kernel(after, pieces, src_ref, *refs):
    o_ref, sem = refs[after], refs[-1]
    step = src_ref.shape[0] // pieces
    moves = [
        pltpu.make_async_copy(
            src_ref.at[pl.ds(k * step, step)], o_ref.at[pl.ds(k * step, step)], sem.at[k]
        )
        for k in range(pieces)
    ]
    for move in moves:
        move.start()
    for move in moves:
        move.wait()


def fetch(weight, after):
    src = pltpu.with_memory_space_constraint(weight, pltpu.HBM)
    hbm = pl.BlockSpec(memory_space=pl.ANY)
    pieces = 8
    return pl.pallas_call(
        functools.partial(fetch_kernel, len(after), pieces),
        in_specs=[hbm] * (1 + len(after)),
        out_specs=pl.BlockSpec(memory_space=pltpu.VMEM),
        out_shape=pltpu.VMEM(weight.shape, weight.dtype),
        scratch_shapes=[pltpu.SemaphoreType.DMA((pieces,))],
        cost_estimate=cost(0, 2 * weight.size),
        compiler_params=pltpu.CompilerParams(vmem_limit_bytes=1 * MIB),
    )(src, *after)


def half_of(where_ref, flip, length):
    return pl.ds(pl.multiple_of((where_ref[1] ^ flip) * length, 128), length)


def product_kernel(flip, where_ref, *refs):
    block_refs, (w_ref, o_ref, x_buf) = refs[:-3], refs[-3:]
    count = block_refs[0].shape[0]
    for k, block_ref in enumerate(block_refs):
        at = pl.multiple_of((where_ref[0] ^ k) * count, count)
        x_buf[pl.ds(at, count), :] = block_ref[...]
    cols = half_of(where_ref, flip, o_ref.shape[1])
    o_ref[...] = jnp.dot(x_buf[...], w_ref[:, cols], preferred_element_type=F32).astype(BF16)


def product(where, blocks, w, flip):
    wide = w.shape[1] // 2
    count, deep = blocks[0].shape
    rows = count * len(blocks)
    vmem = pl.BlockSpec(memory_space=pltpu.VMEM)
    return pl.pallas_call(
        functools.partial(product_kernel, flip),
        in_specs=[pl.BlockSpec(memory_space=pltpu.SMEM)] + [vmem] * (len(blocks) + 1),
        out_specs=vmem,
        out_shape=jax.ShapeDtypeStruct((rows, wide), BF16),
        scratch_shapes=[pltpu.VMEM((rows, deep), BF16)],
        cost_estimate=cost(2 * rows * deep * wide, 2 * deep * wide),
        compiler_params=pltpu.CompilerParams(vmem_limit_bytes=4 * MIB),
    )(where, *blocks, w)


def middle_kernel(flip, where_ref, attn_ref, res_ref, gain_ref, *o_refs):
    mid_ref, normed_ref, sq_ref = o_refs
    steps, seqs, _ = res_ref.shape
    rows, wide = mid_ref.shape
    count = rows // (steps * 4)
    cols = half_of(where_ref, flip, wide)
    parts = []
    for d in range(4):
        for s in range(steps):
            parts.append(res_ref[s, d * count : (d + 1) * count, cols].astype(F32))
    mid = (jnp.concatenate(parts, axis=0) + attn_ref[...].astype(F32)).astype(BF16)
    whole = mid.astype(F32)
    mid_ref[...] = mid
    normed_ref[...] = (whole * gain_ref[:1, cols].astype(F32)).astype(BF16)
    sq_ref[...] = jnp.broadcast_to(jnp.sum(whole * whole, axis=1, keepdims=True), sq_ref.shape)


def middle_part(where, flip, attn, residual, gain):
    rows, wide = attn.shape
    vmem = pl.BlockSpec(memory_space=pltpu.VMEM)
    return pl.pallas_call(
        functools.partial(middle_kernel, flip),
        in_specs=[pl.BlockSpec(memory_space=pltpu.SMEM)] + [vmem] * 3,
        out_specs=[vmem] * 3,
        out_shape=[
            jax.ShapeDtypeStruct((rows, wide), BF16),
            jax.ShapeDtypeStruct((rows, wide), BF16),
            jax.ShapeDtypeStruct((rows, 128), F32),
        ],
        cost_estimate=cost(8 * rows * wide, 8 * rows * wide),
        compiler_params=pltpu.CompilerParams(vmem_limit_bytes=6 * MIB),
    )(where, attn, residual, gain)


def first_kernel(wide, where_ref, x_ref, g_ref, u_ref, o_ref):
    deep = half_of(where_ref, 0, x_ref.shape[1])
    length = g_ref.shape[1]
    for k, w_ref in enumerate((g_ref, u_ref)):
        for at in range(0, length, wide):
            here = slice(at, at + wide)
            out = jnp.dot(x_ref[...], w_ref[deep, here], preferred_element_type=F32)
            o_ref[:, k * length + at : k * length + at + wide] = out


def gate_up_first(where, x, weights):
    rows, deep = x.shape
    length = weights[0].shape[1]
    vmem = pl.BlockSpec(memory_space=pltpu.VMEM)
    return pl.pallas_call(
        functools.partial(first_kernel, length // 7),
        in_specs=[pl.BlockSpec(memory_space=pltpu.SMEM)] + [vmem] * 3,
        out_specs=vmem,
        out_shape=jax.ShapeDtypeStruct((rows, 2 * length), F32),
        cost_estimate=cost(4 * rows * deep * length, 4 * deep * length),
        compiler_params=pltpu.CompilerParams(vmem_limit_bytes=4 * MIB),
    )(where, x, *weights)


def second_kernel(chip, groups, where_ref, x_ref, f_ref, g_ref, u_ref, *refs):
    give_refs, (keep_ref, buf) = refs[:groups], refs[groups:]
    me = where_ref[0]
    deep = half_of(where_ref, 1, x_ref.shape[1])
    length = g_ref.shape[1]
    own = length // 4
    rows = give_refs[0].shape[0]
    start = pl.multiple_of(((me // 2) ^ chip) * (2 * own), 128)
    for k, w_ref in enumerate((g_ref, u_ref)):
        out = jnp.dot(x_ref[...], w_ref[deep, pl.ds(start, 2 * own)], preferred_element_type=F32)
        buf[...] = out + f_ref[:, pl.ds(pl.multiple_of(k * length + start, 128), 2 * own)]
        mine = pl.ds(pl.multiple_of((me % 2) * own, 128), own)
        other = pl.ds(pl.multiple_of((1 - me % 2) * own, 128), own)
        here = slice(k * own, (k + 1) * own)
        keep_ref[:, here] = buf[:, mine]
        for n, give_ref in enumerate(give_refs):
            give_ref[:, here] = buf[n * rows : (n + 1) * rows, other].astype(BF16)


def gate_up_second(where, x, first, weights, chip, groups):
    rows, deep = x.shape
    length = weights[0].shape[1]
    own = length // 4
    vmem = pl.BlockSpec(memory_space=pltpu.VMEM)
    *give, keep = pl.pallas_call(
        functools.partial(second_kernel, chip, groups),
        in_specs=[pl.BlockSpec(memory_space=pltpu.SMEM)] + [vmem] * 4,
        out_specs=[vmem] * (groups + 1),
        out_shape=[jax.ShapeDtypeStruct((rows // groups, 2 * own), BF16)] * groups
        + [jax.ShapeDtypeStruct((rows, 2 * own), F32)],
        scratch_shapes=[pltpu.VMEM((rows, 2 * own), F32)],
        cost_estimate=cost(4 * rows * deep * 2 * own, 8 * deep * own),
        compiler_params=pltpu.CompilerParams(vmem_limit_bytes=6 * MIB),
    )(where, x, first, *weights)
    return give, keep


def relay_kernel(n, keep_ref, got_ref, o_ref):
    rows = got_ref.shape[0]
    here = slice(n * rows, (n + 1) * rows)
    o_ref[...] = (keep_ref[here, :] + got_ref[...].astype(F32)).astype(BF16)


def relay(n, keep, got):
    vmem = pl.BlockSpec(memory_space=pltpu.VMEM)
    return pl.pallas_call(
        functools.partial(relay_kernel, n),
        in_specs=[vmem] * 2,
        out_specs=vmem,
        out_shape=jax.ShapeDtypeStruct(got.shape, BF16),
        cost_estimate=cost(got.size, 4 * got.size),
        compiler_params=pltpu.CompilerParams(vmem_limit_bytes=2 * MIB),
    )(keep, got)


def act_kernel(n, full, near_ref, got_ref, far_ref, *refs):
    sq_refs, o_ref = refs[:-1], refs[-1]
    rows, cols = o_ref.shape
    total = functools.reduce(jnp.add, [sq[n * rows : (n + 1) * rows, :1] for sq in sq_refs])
    inv_norm = lax.rsqrt(total / full + 1e-05)
    here = slice(n * rows, (n + 1) * rows)
    both = near_ref[here, :] + got_ref[...].astype(F32) + far_ref[...].astype(F32)
    gate = both[:, :cols] * inv_norm
    up = both[:, cols:] * inv_norm
    o_ref[...] = (gate / (1.0 + jnp.exp(-gate)) * up).astype(BF16)


def act(n, near, got, far, squares, full):
    rows, both = far.shape
    vmem = pl.BlockSpec(memory_space=pltpu.VMEM)
    return pl.pallas_call(
        functools.partial(act_kernel, n, full),
        in_specs=[vmem] * (3 + len(squares)),
        out_specs=vmem,
        out_shape=jax.ShapeDtypeStruct((rows, both // 2), BF16),
        cost_estimate=cost(8 * rows * both, 8 * rows * both),
        compiler_params=pltpu.CompilerParams(vmem_limit_bytes=4 * MIB),
    )(near, got, far, *squares)


def final_kernel(groups, where_ref, *refs):
    mid_refs, ffn_refs, o_ref = refs[:2], refs[2:-1], refs[-1]
    steps = o_ref.shape[0]
    wide = mid_refs[0].shape[1]
    rows = ffn_refs[0].shape[0]
    count = rows * groups // (steps * 4)
    for flip in range(2):
        cols = half_of(where_ref, flip, wide)
        for n in range(groups):
            here = slice(n * rows, (n + 1) * rows)
            ffn = ffn_refs[2 * n + flip][...].astype(F32)
            out = (mid_refs[flip][here, :].astype(F32) + ffn).astype(BF16)
            for k in range(rows // count):
                d, s = divmod(n * (rows // count) + k, steps)
                o_ref[s, d * count : (d + 1) * count, cols] = out[k * count : (k + 1) * count]


def final(where, mids, groups, shape):
    vmem = pl.BlockSpec(memory_space=pltpu.VMEM)
    flat = [*mids, *(x for group in groups for x in group)]
    return pl.pallas_call(
        functools.partial(final_kernel, len(groups)),
        in_specs=[pl.BlockSpec(memory_space=pltpu.SMEM)] + [vmem] * len(flat),
        out_specs=vmem,
        out_shape=jax.ShapeDtypeStruct(shape, BF16),
        cost_estimate=cost(2 * shape[1] * shape[2], 8 * shape[1] * shape[2]),
        compiler_params=pltpu.CompilerParams(vmem_limit_bytes=12 * MIB),
    )(where, *flat)


def down_kernel(chip, flip, has_sum, where_ref, mine_ref, other_ref, w_ref, *refs):
    o_ref, buf = refs[-2:]
    own = mine_ref.shape[1]
    me = where_ref[0]
    buf[:, pl.ds(pl.multiple_of((me % 2) * own, 128), own)] = mine_ref[...]
    buf[:, pl.ds(pl.multiple_of((1 - me % 2) * own, 128), own)] = other_ref[...]
    at = pl.ds(pl.multiple_of(((me // 2) ^ chip) * (2 * own), 128), 2 * own)
    cols = slice(None) if flip is None else half_of(where_ref, flip, o_ref.shape[1])
    total = jnp.dot(buf[...], w_ref[at, cols], preferred_element_type=F32)
    if has_sum:
        total = total + refs[0][:, cols]
    o_ref[...] = total.astype(o_ref.dtype)


def down(where, mine, other, chip, weight, flip=None, total=None, dtype=F32):
    rows, own = mine.shape
    wide = weight.shape[1] // (1 if flip is None else 2)
    vmem = pl.BlockSpec(memory_space=pltpu.VMEM)
    args = [where, mine, other, weight] + ([] if total is None else [total])
    return pl.pallas_call(
        functools.partial(down_kernel, chip, flip, total is not None),
        in_specs=[pl.BlockSpec(memory_space=pltpu.SMEM)] + [vmem] * (len(args) - 1),
        out_specs=vmem,
        out_shape=jax.ShapeDtypeStruct((rows, wide), dtype),
        scratch_shapes=[pltpu.VMEM((rows, 2 * own), BF16)],
        cost_estimate=cost(4 * rows * own * wide, 4 * own * wide),
        compiler_params=pltpu.CompilerParams(vmem_limit_bytes=4 * MIB),
    )(*args)


def pairs(size, step):
    return [(i, i ^ step) for i in range(size)]


def in_order(mine, other, bit, axis=0):
    first = jnp.where(bit == 0, mine, other)
    second = jnp.where(bit == 0, other, mine)
    return jnp.concatenate((first, second), axis=axis)


def levels(size):
    return [1 << k for k in range(size.bit_length() - 1)]


def sum_tensor(send, keep, during=None):
    held = total_of(keep, lax.ppermute(send, "tensor", pairs(4, 1)))
    got = lax.ppermute(held, "tensor", pairs(4, 2))
    beside = None if during is None else during(held)
    if beside is not None:
        got, beside = lax.optimization_barrier((got, beside))
    return total_of(held, got), beside


def gather_rows(block, size):
    me = lax.axis_index("dp")
    count, deep = block.shape
    for step in reversed(levels(size)):
        bit = (me // step) % 2
        block = in_order(block, lax.ppermute(block, "dp", pairs(size, step)), bit)
    block = block.reshape(size, count, deep)
    order = []
    for d in range(size):
        place = 0
        for step in levels(size):
            place = place * 2 + (d // step) % 2
        order.append(block[place])
    return jnp.concatenate(order, axis=0)


def sum_dp(value, size):
    for step in levels(size):
        value = value + lax.ppermute(value, "dp", pairs(size, step))
    return value


def activate(both, inv_norm):
    cols = both.shape[1] // 2
    gate = both[:, :cols] * inv_norm
    up = both[:, cols:] * inv_norm
    return (jax.nn.silu(gate) * up).astype(BF16)


def middle(resid, attn, norm_gain, dp):
    mid = add(resid, attn)
    wide = mid.astype(F32)
    squares = sum_dp(jnp.sum(wide * wide, axis=1)[None, :], dp)
    inv_norm = lax.rsqrt(squares / (mid.shape[1] * dp) + 1e-05).reshape(mid.shape[0], 1)
    normed = (wide * norm_gain.astype(F32)[None, :]).astype(BF16)
    return mid, inv_norm, normed


def plain(rows, resid, out_weight, norm_gain, gate_weight, up_weight, down_weight, dp):
    part = jnp.dot(rows, out_weight, preferred_element_type=F32).astype(BF16)
    mid, inv_norm, normed = middle(resid, lax.psum(part, "tensor"), norm_gain, dp)
    both = []
    for weight in (gate_weight, up_weight):
        term = jnp.dot(normed, weight, preferred_element_type=F32).astype(BF16)
        both.append(lax.psum_scatter(term, "dp", scatter_dimension=1, tiled=True).astype(F32))
    hidden = activate(jnp.concatenate(both, axis=1), inv_norm)
    hidden = lax.all_gather(hidden, "dp", axis=1, tiled=True)
    part = jnp.dot(hidden, down_weight, preferred_element_type=F32).astype(BF16)
    return add(mid, lax.psum(part, "tensor"))


def body(
    residual,
    queries,
    new_keys,
    new_values,
    key_cache,
    value_cache,
    lengths,
    out_weight,
    norm_gain,
    gate_weight,
    up_weight,
    down_weight,
):
    dp = lax.axis_size("dp")
    tensor = lax.axis_size("tensor")
    steps, all_seqs, width = residual.shape
    local_seqs = queries.shape[1]
    where = jnp.stack([lax.axis_index("dp"), lax.axis_index("tensor") % 2])
    where, lengths = lax.optimization_barrier((where, lengths))
    heads, out_w = attention(
        queries, new_keys, new_values, key_cache, value_cache, lengths, out_weight
    )
    if dp == 4 and tensor == 4:
        weights = gate_weight, up_weight, down_weight
        gain, heads = lax.optimization_barrier((norm_gain, heads))
        return fast(where, heads, residual, gain, out_w, *weights)
    row_count = steps * all_seqs
    resid = residual.reshape(steps, dp, local_seqs, width).swapaxes(0, 1)
    weights = out_w, norm_gain, gate_weight, up_weight, down_weight
    out = plain(gather_rows(heads, dp), resid.reshape(row_count, width), *weights, dp)
    return out.reshape(dp, steps, local_seqs, width).swapaxes(0, 1).reshape(residual.shape)


def fast(where, heads, residual, gain, out_w, gate_weight, up_weight, down_weight):
    width = out_w.shape[1]
    groups = 2
    core = lambda value: lax.ppermute(value, "dp", pairs(4, 1))
    across = lambda value: lax.ppermute(value, "dp", pairs(4, 2))
    swap = lambda value: lax.ppermute(value, "tensor", pairs(4, 1))
    gain = jnp.broadcast_to(gain[None, :], (16, width))
    far = across(heads)
    blocks = [heads, core(heads), far, core(far)]
    blocks, gain = lax.optimization_barrier((blocks, gain))
    send = product(where, blocks, out_w, 1)
    keep = product(where, blocks, out_w, 0)
    gate_w = fetch(gate_weight, [keep])
    got = swap(send)
    got, gate_w = lax.optimization_barrier((got, gate_w))
    held = total_of(keep, got)
    got = lax.ppermute(held, "tensor", pairs(4, 2))
    up_w = fetch(up_weight, [held])
    got, up_w = lax.optimization_barrier((got, up_w))
    held = total_of(held, got)
    other = swap(held)
    weights = gate_w, up_w
    mid, normed, sq = middle_part(where, 0, held, residual, gain)
    first = gate_up_first(where, normed, weights)
    other, first = lax.optimization_barrier((other, first))
    mid_other, normed, sq_other = middle_part(where, 1, other, residual, gain)
    sq = total_of(sq, sq_other, dtype=F32)
    sq_far = across(sq)
    normed, sq_core = lax.optimization_barrier((normed, core(sq)))
    give, keep = gate_up_second(where, normed, first, weights, 1, groups)
    far = [core(x) for x in give]
    far, sq_far = lax.optimization_barrier((far, sq_far))
    squares = [sq, sq_core, sq_far, core(sq_far)]
    relayed = [relay(n, keep, x) for n, x in enumerate(far)]
    far = [across(x) for x in relayed]
    normed, relayed = lax.optimization_barrier((normed, relayed))
    give, near = gate_up_second(where, normed, first, weights, 0, groups)
    got = [core(x) for x in give]
    down_w = fetch(down_weight, [near])
    far[0], down_w = lax.optimization_barrier((far[0], down_w))
    mine, mine_far, other, totals, outs = [], [], [], [], []
    for n in range(groups):
        if n:
            far[n], totals[0] = lax.optimization_barrier((far[n], totals[0]))
        mine.append(act(n, near, got[n], far[n], squares, width * 4))
        mine_far.append(across(mine[n]))
        other.append(core(mine[n]))
        totals.append(down(where, mine[n], other[n], 0, down_w))
    for n in range(groups):
        last = lambda flip: down(
            where, mine_far[n], other_far, 1, down_w, flip, totals[n], BF16
        )
        if n:
            mine_far[n], send = lax.optimization_barrier((mine_far[n], send))
        other_far = core(mine_far[n])
        send = last(1)
        keep = last(0)
        held, _ = sum_tensor(send, keep)
        outs.append((held, swap(held)))
    return final(where, [mid, mid_other], outs, residual.shape)


def solution(mesh):
    in_specs = (
        P(None, "replica", "dp"),
        P(None, ("replica", "dp"), "tensor"),
        P(None, ("replica", "dp"), "tensor", None),
        P(None, ("replica", "dp"), "tensor", None),
        P(("replica", "dp"), "tensor", None, None),
        P(("replica", "dp"), "tensor", None, None),
        P(("replica", "dp")),
        P("tensor", "dp"),
        P("dp"),
        P("dp", "tensor"),
        P("dp", "tensor"),
        P("tensor", "dp"),
    )
    out_specs = P(None, "replica", "dp")
    return jax.shard_map(body, mesh=mesh, in_specs=in_specs, out_specs=out_specs, check_vma=False)
```

```python
import functools

import jax
import jax.numpy as jnp
from jax import lax
from jax.experimental import pallas as pl
from jax.experimental.pallas import tpu as pltpu
from jax.sharding import PartitionSpec as P

BF16 = jnp.bfloat16
F32 = jnp.float32
MIB = 1 << 20


def add(a, b):
    return (a.astype(F32) + b.astype(F32)).astype(BF16)


def sum_kernel(dtype, *refs):
    total = functools.reduce(jnp.add, [ref[...].astype(F32) for ref in refs[:-1]])
    refs[-1][...] = total.astype(dtype)


def total_of(*terms, dtype=BF16):
    vmem = pl.BlockSpec(memory_space=pltpu.VMEM)
    return pl.pallas_call(
        functools.partial(sum_kernel, dtype),
        in_specs=[vmem] * len(terms),
        out_specs=vmem,
        out_shape=jax.ShapeDtypeStruct(terms[0].shape, dtype),
        cost_estimate=cost(terms[0].size, 4 * terms[0].size),
        compiler_params=pltpu.CompilerParams(vmem_limit_bytes=2 * MIB),
    )(*terms)


def cost(flops, read):
    return pl.CostEstimate(flops=flops // 1000, bytes_accessed=read // 1000, transcendentals=0)


def attention_kernel(first, count, len_hbm, q_hbm, k_hbm, v_hbm, nk_hbm, nv_hbm, *refs):
    o_ref, len_ref, q_ref, nk_ref, nv_ref = refs[:5]
    k_buf, v_buf, out_buf, sem, small_sem = refs[5:]
    ends = ((len_hbm, len_ref), (q_hbm, q_ref), (nk_hbm, nk_ref), (nv_hbm, nv_ref))
    small = [
        pltpu.make_async_copy(src, dst, small_sem.at[k]) for k, (src, dst) in enumerate(ends)
    ]
    for move in small:
        move.start()
    steps = q_ref.shape[0]
    _, copies, slots, head = k_hbm.shape
    group = q_ref.shape[2] // (copies * head)
    rows = steps * group
    part = 256
    parts = slots // part
    batch = 4
    scaling = head ** (-0.5)

    def moves(b, c):
        here = pl.ds(c * part, part)
        return (
            pltpu.make_async_copy(k_hbm.at[first + b, :, here], k_buf.at[b, :, here], sem.at[0, b]),
            pltpu.make_async_copy(v_hbm.at[first + b, :, here], v_buf.at[b, :, here], sem.at[1, b]),
        )

    def start(b, c):
        for move in moves(b, c):
            move.start()

    def clear(b, c):
        v_buf[b, :, c * part : (c + 1) * part] = jnp.zeros((copies, part, head), BF16)

    def wait(b, c):
        for move in moves(b, c):
            move.wait()

    start(0, 0)
    small[0].wait()
    for b in range(count):
        if b:
            start(b, 0)
        for c in range(1, parts):
            live = len_ref[first + b] > c * part
            pl.when(live)(functools.partial(start, b, c))
            pl.when(jnp.logical_not(live))(functools.partial(clear, b, c))

    for move in small[1:]:
        move.wait()
    slot = lax.broadcasted_iota(jnp.int32, (rows, slots), 1)
    step = lax.broadcasted_iota(jnp.int32, (rows, 1), 0) // group
    for b0 in range(0, count, batch):
        work = [(b, g) for b in range(b0, min(b0 + batch, count)) for g in range(copies)]
        asked, recent = [], []
        for b, g in work:
            pick = [
                q_ref[s, first + b : first + b + 1, (g * group + j) * head : (g * group + j + 1) * head]
                for s in range(steps)
                for j in range(group)
            ]
            wide = jnp.concatenate([p.astype(F32) for p in pick], axis=0)
            asked.append(wide.astype(BF16))
            found = []
            for r in range(steps):
                key = nk_ref[r, first + b, g : g + 1, :].astype(F32)
                score = jnp.sum(wide * key, axis=1, keepdims=True) * scaling
                found.append(jnp.where(step >= r, score, -jnp.inf))
            recent.append(found)
        for b in range(b0, min(b0 + batch, count)):
            wait(b, 0)
            for c in range(1, parts):
                pl.when(len_ref[first + b] > c * part)(functools.partial(wait, b, c))
        scores = [
            lax.dot_general(q, k_buf[b, g], (((1,), (1,)), ((), ())), preferred_element_type=F32)
            for q, (b, g) in zip(asked, work)
        ]
        scores = [
            jnp.where(slot < len_ref[first + b], s * scaling, -jnp.inf)
            for s, (b, g) in zip(scores, work)
        ]
        tops = [
            functools.reduce(jnp.maximum, [jnp.max(s, axis=1, keepdims=True)] + found)
            for s, found in zip(scores, recent)
        ]
        weights = [jnp.exp(s - top) for s, top in zip(scores, tops)]
        fresh = [[jnp.exp(x - top) for x in found] for found, top in zip(recent, tops)]
        totals = [jnp.sum(w, axis=1, keepdims=True) + sum(f) for w, f in zip(weights, fresh)]
        blends = [
            jnp.dot(w.astype(BF16), v_buf[b, g], preferred_element_type=F32)
            for w, (b, g) in zip(weights, work)
        ]
        for (b, g), blend, f, total in zip(work, blends, fresh, totals):
            for r in range(steps):
                value = nv_ref[r, first + b, g : g + 1, :].astype(F32)
                blend = blend + f[r].astype(BF16).astype(F32) * value
            out = blend / total
            for s in range(steps):
                for j in range(group):
                    cols = slice((g * group + j) * head, (g * group + j + 1) * head)
                    at = s * count + b
                    out_buf[at : at + 1, cols] = out[s * group + j : s * group + j + 1, :]
    o_ref[...] = out_buf[...].astype(BF16)


def attention(queries, new_keys, new_values, key_cache, value_cache, lengths):
    first, count = 0, queries.shape[1]
    steps, _, deep = queries.shape
    _, copies, slots, head = key_cache.shape
    vmem = pl.BlockSpec(memory_space=pltpu.VMEM)
    hbm = pl.BlockSpec(memory_space=pl.ANY)
    buffer = pltpu.VMEM((count, copies, slots, head), BF16)
    moved = [lengths, queries, key_cache, value_cache, new_keys, new_values]
    moved = [pltpu.with_memory_space_constraint(x, pltpu.HBM) for x in moved]
    return pl.pallas_call(
        functools.partial(attention_kernel, first, count),
        in_specs=[hbm] * 6,
        out_specs=vmem,
        out_shape=jax.ShapeDtypeStruct((steps * count, deep), BF16),
        scratch_shapes=[
            pltpu.SMEM(lengths.shape, lengths.dtype),
            pltpu.VMEM(queries.shape, BF16),
            pltpu.VMEM(new_keys.shape, BF16),
            pltpu.VMEM(new_values.shape, BF16),
            buffer,
            buffer,
            pltpu.VMEM((steps * count, deep), F32),
            pltpu.SemaphoreType.DMA((2, count)),
            pltpu.SemaphoreType.DMA((4,)),
        ],
        cost_estimate=cost(4 * steps * count * slots * deep, 4 * count * copies * slots * head),
        compiler_params=pltpu.CompilerParams(vmem_limit_bytes=20 * MIB),
    )(*moved)


def fetch_kernel(axis, flip, pieces, where_ref, src_ref, *refs):
    o_ref, sem = refs[-2:]
    cut = [pl.ds(0, n) for n in src_ref.shape]
    cut[axis] = half_of(where_ref, flip, o_ref.shape[axis])
    if axis == 0:
        start, step = cut[0].start, o_ref.shape[0] // pieces
    else:
        start, step = 0, src_ref.shape[0] // pieces
    moves = []
    for k in range(pieces):
        from_ref = src_ref.at[pl.ds(pl.multiple_of(start + k * step, 16), step), cut[1]]
        moves.append(
            pltpu.make_async_copy(from_ref, o_ref.at[pl.ds(k * step, step)], sem.at[k])
        )
    for move in moves:
        move.start()
    for move in moves:
        move.wait()


def fetch(where, weight, axis, flip, after):
    src = pltpu.with_memory_space_constraint(weight, pltpu.HBM)
    hbm = pl.BlockSpec(memory_space=pl.ANY)
    pieces = 8
    shape = list(weight.shape)
    shape[axis] //= 2
    return pl.pallas_call(
        functools.partial(fetch_kernel, axis, flip, pieces),
        in_specs=[pl.BlockSpec(memory_space=pltpu.SMEM)] + [hbm] * (1 + len(after)),
        out_specs=pl.BlockSpec(memory_space=pltpu.VMEM),
        out_shape=pltpu.VMEM(tuple(shape), weight.dtype),
        scratch_shapes=[pltpu.SemaphoreType.DMA((pieces,))],
        cost_estimate=cost(0, weight.size),
        compiler_params=pltpu.CompilerParams(vmem_limit_bytes=1 * MIB),
    )(where, src, *after)


def half_of(where_ref, flip, length):
    return pl.ds(pl.multiple_of((where_ref[1] ^ flip) * length, 128), length)


def product_kernel(flip, groups, where_ref, *refs):
    x_buf, o_refs = refs[-1], refs[-1 - groups : -1]
    block_refs, w_ref = refs[: -2 - groups], refs[-2 - groups]
    count = block_refs[0].shape[0]
    for k, block_ref in enumerate(block_refs):
        at = pl.multiple_of((where_ref[0] ^ k) * count, count)
        x_buf[pl.ds(at, count), :] = block_ref[...]
    rows, wide = o_refs[0].shape
    cols = half_of(where_ref, flip, wide)
    out = jnp.dot(x_buf[...], w_ref[:, cols], preferred_element_type=F32).astype(BF16)
    for n, o_ref in enumerate(o_refs):
        o_ref[...] = out[n * rows : (n + 1) * rows]


def product(where, blocks, w, flip, groups):
    wide = w.shape[1] // 2
    count, deep = blocks[0].shape
    rows = count * len(blocks)
    vmem = pl.BlockSpec(memory_space=pltpu.VMEM)
    return pl.pallas_call(
        functools.partial(product_kernel, flip, groups),
        in_specs=[pl.BlockSpec(memory_space=pltpu.SMEM)] + [vmem] * (len(blocks) + 1),
        out_specs=[vmem] * groups,
        out_shape=[jax.ShapeDtypeStruct((rows // groups, wide), BF16)] * groups,
        scratch_shapes=[pltpu.VMEM((rows, deep), BF16)],
        cost_estimate=cost(2 * rows * deep * wide, 2 * deep * wide),
        compiler_params=pltpu.CompilerParams(vmem_limit_bytes=4 * MIB),
    )(where, *blocks, w)


def middle_kernel(flip, groups, where_ref, *refs):
    attn_refs, (res_ref, gain_ref, mid_ref, normed_ref) = refs[:groups], refs[groups : groups + 4]
    steps = res_ref.shape[0]
    rows, wide = mid_ref.shape
    count = rows // (steps * 4)
    cols = half_of(where_ref, flip, wide)
    parts = []
    for d in range(4):
        for s in range(steps):
            parts.append(res_ref[s, d * count : (d + 1) * count, cols].astype(F32))
    attn = jnp.concatenate([ref[...].astype(F32) for ref in attn_refs], axis=0)
    mid = (jnp.concatenate(parts, axis=0) + attn).astype(BF16)
    whole = mid.astype(F32)
    mid_ref[...] = mid
    normed_ref[...] = (whole * gain_ref[:1, cols].astype(F32)).astype(BF16)
    for sq_ref in refs[groups + 4 :]:
        squares = jnp.broadcast_to(jnp.sum(whole * whole, axis=1, keepdims=True), (rows, rows))
        sq_ref[...] = jnp.transpose(squares)[: sq_ref.shape[0]]


def middle_part(where, flip, attn, residual, gain):
    rows, wide = attn[0].shape[0] * len(attn), attn[0].shape[1]
    vmem = pl.BlockSpec(memory_space=pltpu.VMEM)
    outs = [jax.ShapeDtypeStruct((rows, wide), BF16)] * 2
    if not flip:
        outs.append(jax.ShapeDtypeStruct((8, rows), F32))
    return pl.pallas_call(
        functools.partial(middle_kernel, flip, len(attn)),
        in_specs=[pl.BlockSpec(memory_space=pltpu.SMEM)] + [vmem] * (len(attn) + 2),
        out_specs=[vmem] * len(outs),
        out_shape=outs,
        cost_estimate=cost(8 * rows * wide, 8 * rows * wide),
        compiler_params=pltpu.CompilerParams(vmem_limit_bytes=6 * MIB),
    )(where, *attn, residual, gain)


def first_kernel(wide, where_ref, x_ref, g_ref, u_ref, o_ref):
    deep, all_rows = half_of(where_ref, 0, x_ref.shape[1]), slice(None)
    length = g_ref.shape[1]
    for k, w_ref in enumerate((g_ref, u_ref)):
        for at in range(0, length, wide):
            here = slice(at, at + wide)
            out = jnp.dot(x_ref[...], w_ref[deep if k else all_rows, here], preferred_element_type=F32)
            o_ref[:, k * length + at : k * length + at + wide] = out


def gate_up_first(where, x, weights):
    rows, deep = x.shape
    length = weights[0].shape[1]
    vmem = pl.BlockSpec(memory_space=pltpu.VMEM)
    return pl.pallas_call(
        functools.partial(first_kernel, length // 7),
        in_specs=[pl.BlockSpec(memory_space=pltpu.SMEM)] + [vmem] * 3,
        out_specs=vmem,
        out_shape=jax.ShapeDtypeStruct((rows, 2 * length), F32),
        cost_estimate=cost(4 * rows * deep * length, 4 * deep * length),
        compiler_params=pltpu.CompilerParams(vmem_limit_bytes=4 * MIB),
    )(where, x, *weights)


def second_kernel(chip, groups, where_ref, x_ref, f_ref, g_ref, u_ref, *refs):
    give_refs, (keep_ref, buf) = refs[:groups], refs[groups:]
    me = where_ref[0]
    deep, all_rows = half_of(where_ref, 1, x_ref.shape[1]), slice(None)
    length = g_ref.shape[1]
    own = length // 4
    rows = give_refs[0].shape[0]
    start = pl.multiple_of(((me // 2) ^ chip) * (2 * own), 128)
    for k, w_ref in enumerate((g_ref, u_ref)):
        out = jnp.dot(x_ref[...], w_ref[deep if k else all_rows, pl.ds(start, 2 * own)], preferred_element_type=F32)
        buf[...] = out + f_ref[:, pl.ds(pl.multiple_of(k * length + start, 128), 2 * own)]
        mine = pl.ds(pl.multiple_of((me % 2) * own, 128), own)
        other = pl.ds(pl.multiple_of((1 - me % 2) * own, 128), own)
        here = slice(k * own, (k + 1) * own)
        keep_ref[:, here] = buf[:, mine]
        for n, give_ref in enumerate(give_refs):
            give_ref[:, here] = buf[n * rows : (n + 1) * rows, other].astype(BF16)


def gate_up_second(where, x, first, weights, chip, groups):
    rows, deep = x.shape
    length = weights[0].shape[1]
    own = length // 4
    vmem = pl.BlockSpec(memory_space=pltpu.VMEM)
    *give, keep = pl.pallas_call(
        functools.partial(second_kernel, chip, groups),
        in_specs=[pl.BlockSpec(memory_space=pltpu.SMEM)] + [vmem] * 4,
        out_specs=[vmem] * (groups + 1),
        out_shape=[jax.ShapeDtypeStruct((rows // groups, 2 * own), BF16)] * groups
        + [jax.ShapeDtypeStruct((rows, 2 * own), F32)],
        scratch_shapes=[pltpu.VMEM((rows, 2 * own), F32)],
        cost_estimate=cost(4 * rows * deep * 2 * own, 8 * deep * own),
        compiler_params=pltpu.CompilerParams(vmem_limit_bytes=6 * MIB),
    )(where, x, first, *weights)
    return give, keep


def relay_kernel(n, keep_ref, got_ref, o_ref):
    rows = got_ref.shape[0]
    here = slice(n * rows, (n + 1) * rows)
    o_ref[...] = (keep_ref[here, :] + got_ref[...].astype(F32)).astype(BF16)


def relay(n, keep, got):
    vmem = pl.BlockSpec(memory_space=pltpu.VMEM)
    return pl.pallas_call(
        functools.partial(relay_kernel, n),
        in_specs=[vmem] * 2,
        out_specs=vmem,
        out_shape=jax.ShapeDtypeStruct(got.shape, BF16),
        cost_estimate=cost(got.size, 4 * got.size),
        compiler_params=pltpu.CompilerParams(vmem_limit_bytes=2 * MIB),
    )(keep, got)


def act_kernel(n, full, near_ref, got_ref, far_ref, *refs):
    sq_refs, o_ref = refs[:-1], refs[-1]
    rows, cols = o_ref.shape
    total = functools.reduce(jnp.add, [sq[:1, :] for sq in sq_refs])
    total = jnp.transpose(jnp.broadcast_to(total, (total.shape[1], total.shape[1])))
    total = total[n * rows : (n + 1) * rows, :1]
    inv_norm = lax.rsqrt(total / full + 1e-05)
    here = slice(n * rows, (n + 1) * rows)
    both = near_ref[here, :] + got_ref[...].astype(F32) + far_ref[...].astype(F32)
    gate = both[:, :cols] * inv_norm
    up = both[:, cols:] * inv_norm
    o_ref[...] = (gate / (1.0 + jnp.exp(-gate)) * up).astype(BF16)


def act(n, near, got, far, squares, full):
    rows, both = far.shape
    vmem = pl.BlockSpec(memory_space=pltpu.VMEM)
    return pl.pallas_call(
        functools.partial(act_kernel, n, full),
        in_specs=[vmem] * (3 + len(squares)),
        out_specs=vmem,
        out_shape=jax.ShapeDtypeStruct((rows, both // 2), BF16),
        cost_estimate=cost(8 * rows * both, 8 * rows * both),
        compiler_params=pltpu.CompilerParams(vmem_limit_bytes=4 * MIB),
    )(near, got, far, *squares)


def final_kernel(groups, where_ref, *refs):
    mid_refs, ffn_refs, o_ref = refs[:2], refs[2:-1], refs[-1]
    steps = o_ref.shape[0]
    wide = mid_refs[0].shape[1]
    rows = ffn_refs[0].shape[0]
    count = rows * groups // (steps * 4)
    for flip in range(2):
        cols = half_of(where_ref, flip, wide)
        for n in range(groups):
            here = slice(n * rows, (n + 1) * rows)
            ffn = ffn_refs[2 * n + flip][...].astype(F32)
            out = (mid_refs[flip][here, :].astype(F32) + ffn).astype(BF16)
            for k in range(rows // count):
                d, s = divmod(n * (rows // count) + k, steps)
                o_ref[s, d * count : (d + 1) * count, cols] = out[k * count : (k + 1) * count]


def final(where, mids, groups, shape):
    vmem = pl.BlockSpec(memory_space=pltpu.VMEM)
    flat = [*mids, *(x for group in groups for x in group)]
    return pl.pallas_call(
        functools.partial(final_kernel, len(groups)),
        in_specs=[pl.BlockSpec(memory_space=pltpu.SMEM)] + [vmem] * len(flat),
        out_specs=vmem,
        out_shape=jax.ShapeDtypeStruct(shape, BF16),
        cost_estimate=cost(2 * shape[1] * shape[2], 8 * shape[1] * shape[2]),
        compiler_params=pltpu.CompilerParams(vmem_limit_bytes=12 * MIB),
    )(where, *flat)


def down_kernel(chip, flip, where_ref, mine_ref, other_ref, w_ref, *refs):
    o_ref, buf = refs[-2:]
    own = mine_ref.shape[1]
    me = where_ref[0]
    buf[:, pl.ds(pl.multiple_of((me % 2) * own, 128), own)] = mine_ref[...]
    buf[:, pl.ds(pl.multiple_of((1 - me % 2) * own, 128), own)] = other_ref[...]
    at = pl.ds(pl.multiple_of(((me // 2) ^ chip) * (2 * own), 128), 2 * own)
    total = jnp.dot(buf[...], w_ref[at, half_of(where_ref, flip, o_ref.shape[1])], preferred_element_type=F32)
    for ref in refs[:-2]:
        total = total + ref[...]
    o_ref[...] = total.astype(o_ref.dtype)


def down(where, mine, other, chip, weight, flip, total=None):
    rows, own = mine.shape
    wide = weight.shape[1] // 2
    dtype = F32 if total is None else BF16
    vmem = pl.BlockSpec(memory_space=pltpu.VMEM)
    args = [where, mine, other, weight] + ([] if total is None else [total])
    return pl.pallas_call(
        functools.partial(down_kernel, chip, flip),
        in_specs=[pl.BlockSpec(memory_space=pltpu.SMEM)] + [vmem] * (len(args) - 1),
        out_specs=vmem,
        out_shape=jax.ShapeDtypeStruct((rows, wide), dtype),
        scratch_shapes=[pltpu.VMEM((rows, 2 * own), BF16)],
        cost_estimate=cost(4 * rows * own * wide, 4 * own * wide),
        compiler_params=pltpu.CompilerParams(vmem_limit_bytes=4 * MIB),
    )(*args)


def pairs(size, step):
    return [(i, i ^ step) for i in range(size)]


def in_order(mine, other, bit, axis=0):
    first = jnp.where(bit == 0, mine, other)
    second = jnp.where(bit == 0, other, mine)
    return jnp.concatenate((first, second), axis=axis)


def levels(size):
    return [1 << k for k in range(size.bit_length() - 1)]


def gather_rows(block, size):
    me = lax.axis_index("dp")
    count, deep = block.shape
    for step in reversed(levels(size)):
        bit = (me // step) % 2
        block = in_order(block, lax.ppermute(block, "dp", pairs(size, step)), bit)
    block = block.reshape(size, count, deep)
    order = []
    for d in range(size):
        place = 0
        for step in levels(size):
            place = place * 2 + (d // step) % 2
        order.append(block[place])
    return jnp.concatenate(order, axis=0)


def sum_dp(value, size):
    for step in levels(size):
        value = value + lax.ppermute(value, "dp", pairs(size, step))
    return value


def activate(both, inv_norm):
    cols = both.shape[1] // 2
    gate = both[:, :cols] * inv_norm
    up = both[:, cols:] * inv_norm
    return (jax.nn.silu(gate) * up).astype(BF16)


def middle(resid, attn, norm_gain, dp):
    mid = add(resid, attn)
    wide = mid.astype(F32)
    squares = sum_dp(jnp.sum(wide * wide, axis=1)[None, :], dp)
    inv_norm = lax.rsqrt(squares / (mid.shape[1] * dp) + 1e-05).reshape(mid.shape[0], 1)
    normed = (wide * norm_gain.astype(F32)[None, :]).astype(BF16)
    return mid, inv_norm, normed


def plain(rows, resid, out_weight, norm_gain, gate_weight, up_weight, down_weight, dp):
    part = jnp.dot(rows, out_weight, preferred_element_type=F32).astype(BF16)
    mid, inv_norm, normed = middle(resid, lax.psum(part, "tensor"), norm_gain, dp)
    both = []
    for weight in (gate_weight, up_weight):
        term = jnp.dot(normed, weight, preferred_element_type=F32).astype(BF16)
        both.append(lax.psum_scatter(term, "dp", scatter_dimension=1, tiled=True).astype(F32))
    hidden = activate(jnp.concatenate(both, axis=1), inv_norm)
    hidden = lax.all_gather(hidden, "dp", axis=1, tiled=True)
    part = jnp.dot(hidden, down_weight, preferred_element_type=F32).astype(BF16)
    return add(mid, lax.psum(part, "tensor"))


def body(
    residual,
    queries,
    new_keys,
    new_values,
    key_cache,
    value_cache,
    lengths,
    out_weight,
    norm_gain,
    gate_weight,
    up_weight,
    down_weight,
):
    dp = lax.axis_size("dp")
    tensor = lax.axis_size("tensor")
    steps, all_seqs, width = residual.shape
    local_seqs = queries.shape[1]
    where = jnp.stack([lax.axis_index("dp"), lax.axis_index("tensor") % 2])
    where, queries = lax.optimization_barrier((where, queries))
    heads = attention(queries, new_keys, new_values, key_cache, value_cache, lengths)
    if dp == 4 and tensor == 4:
        weights = gate_weight, up_weight, down_weight
        gain, heads = lax.optimization_barrier((norm_gain, heads))
        return fast(where, heads, residual, gain, out_weight, *weights)
    row_count = steps * all_seqs
    resid = residual.reshape(steps, dp, local_seqs, width).swapaxes(0, 1)
    weights = out_weight, norm_gain, gate_weight, up_weight, down_weight
    out = plain(gather_rows(heads, dp), resid.reshape(row_count, width), *weights, dp)
    return out.reshape(dp, steps, local_seqs, width).swapaxes(0, 1).reshape(residual.shape)


def fast(where, heads, residual, gain, out_w, gate_weight, up_weight, down_weight):
    width = out_w.shape[1]
    groups = 2
    core = lambda value: lax.ppermute(value, "dp", pairs(4, 1))
    across = lambda value: lax.ppermute(value, "dp", pairs(4, 2))
    swap = lambda value: lax.ppermute(value, "tensor", pairs(4, 1))
    gain = jnp.broadcast_to(gain[None, :], (16, width))
    after = lambda value, *others: lax.optimization_barrier((value, *others))[0]

    def sum_tensor(sends, keeps, during=lambda n, held: None):
        gots = [swap(send) for send in sends]
        helds, crosses = [None, None], [None, None]
        for n in range(2):
            if n:
                gots[n] = after(gots[n], helds[0])
            keep, gots[n] = keeps(n, helds[0], gots[n])
            helds[n] = total_of(keep, gots[n])
            crosses[n] = lax.ppermute(helds[n], "tensor", pairs(4, 2))
        others = [None, None]
        for n in range(2):
            beside = during(n, helds[1 - n])
            if beside is not None:
                crosses[n] = after(crosses[n], beside)
            helds[n] = total_of(helds[n], crosses[n])
            others[n] = swap(helds[n])
            if n == 0:
                crosses[1] = after(crosses[1], helds[0])
        return helds, others

    out_w, up_w, down_w = [
        pltpu.with_memory_space_constraint(w, pltpu.VMEM) for w in (out_w, up_weight, down_weight)
    ]
    gate_own = fetch(where, gate_weight, 0, 0, [heads])
    far = across(heads)
    near = core(heads)
    far, near, gate_own = lax.optimization_barrier((far, near, gate_own))
    blocks = [heads, near, far, core(far)]
    blocks, gain = lax.optimization_barrier((blocks, gain))
    sends = product(where, blocks, out_w, 1, groups)
    kept = product(where, blocks, out_w, 0, groups)

    gate_far = []

    def keeps(n, held, got):
        return kept[n], got

    def during(n, held):
        if n == 0:
            gate_far.append(fetch(where, gate_weight, 0, 1, [held]))
            return gate_far[0]

    helds, others = sum_tensor(sends, keeps, during)
    mid, normed, sq = middle_part(where, 0, helds, residual, gain)
    sq_core = core(sq)
    first = gate_up_first(where, normed, (gate_own, up_w))
    sq_chip = total_of(sq, sq_core, dtype=F32)
    sq_sum = total_of(sq_chip, across(sq_chip), dtype=F32)
    others, first, sq_sum = lax.optimization_barrier((others, first, sq_sum))
    squares = [sq_sum, swap(sq_sum)]
    mid_other, normed = middle_part(where, 1, others, residual, gain)
    weights = gate_far[0], up_w
    give, keep = gate_up_second(where, normed, first, weights, 1, groups)
    far = [core(x) for x in give]
    relayed = [relay(n, keep, x) for n, x in enumerate(far)]
    far = [across(x) for x in relayed]
    normed, relayed = lax.optimization_barrier((normed, relayed))
    give, near = gate_up_second(where, normed, first, weights, 0, groups)
    got = [core(x) for x in give]
    far[0], near, got = lax.optimization_barrier((far[0], near, got))

    def activated(n):
        mine = act(n, near, got[n], far[n], squares, width * 4)
        other = core(mine)
        return mine, across(mine), other

    def early(n):
        return [down(where, mine[n], other[n], 0, down_w, flip) for flip in (1, 0)]

    mine, mine_far, other, totals, other_far = [0] * 2, [0] * 2, [0] * 2, [0] * 2, [0] * 2
    mine[0], mine_far[0], other[0] = activated(0)
    totals[0] = early(0)
    far[1] = after(far[1], totals[0])
    mine[1], mine_far[1], other[1] = activated(1)
    mine_far[0] = after(mine_far[0], mine[1])
    other_far[0] = core(mine_far[0])
    totals[1] = early(1)
    other_far[0] = after(other_far[0], totals[1])
    send_a = down(where, mine_far[0], other_far[0], 1, down_w, 1, totals[0][0])
    keep_a = down(where, mine_far[0], other_far[0], 1, down_w, 0, totals[0][1])
    mine_far[1] = after(mine_far[1], keep_a)
    other_far[1] = core(mine_far[1])
    send_b = down(where, mine_far[1], other_far[1], 1, down_w, 1, totals[1][0])

    def keeps(n, held, got):
        if n == 0:
            return keep_a, after(got, send_b)
        total = after(totals[1][1], held)
        return down(where, mine_far[1], other_far[1], 1, down_w, 0, total), got

    helds, others = sum_tensor([send_a, send_b], keeps)
    outs = list(zip(helds, others))
    return final(where, [mid, mid_other], outs, residual.shape)


def solution(mesh):
    in_specs = (
        P(None, "replica", "dp"),
        P(None, ("replica", "dp"), "tensor"),
        P(None, ("replica", "dp"), "tensor", None),
        P(None, ("replica", "dp"), "tensor", None),
        P(("replica", "dp"), "tensor", None, None),
        P(("replica", "dp"), "tensor", None, None),
        P(("replica", "dp")),
        P("tensor", "dp"),
        P("dp"),
        P("dp", "tensor"),
        P("dp", "tensor"),
        P("tensor", "dp"),
    )
    out_specs = P(None, "replica", "dp")
    return jax.shard_map(body, mesh=mesh, in_specs=in_specs, out_specs=out_specs, check_vma=False)
```

```python
import functools

import jax
import jax.numpy as jnp
from jax import lax
from jax.experimental import pallas as pl
from jax.experimental.pallas import tpu as pltpu
from jax.sharding import PartitionSpec as P

BF16 = jnp.bfloat16
F32 = jnp.float32
MIB = 1 << 20


def add(a, b):
    return (a.astype(F32) + b.astype(F32)).astype(BF16)


def sum_kernel(dtype, *refs):
    total = functools.reduce(jnp.add, [ref[...].astype(F32) for ref in refs[:-1]])
    refs[-1][...] = total.astype(dtype)


def total_of(*terms, dtype=BF16):
    vmem = pl.BlockSpec(memory_space=pltpu.VMEM)
    return pl.pallas_call(
        functools.partial(sum_kernel, dtype),
        in_specs=[vmem] * len(terms),
        out_specs=vmem,
        out_shape=jax.ShapeDtypeStruct(terms[0].shape, dtype),
        cost_estimate=cost(terms[0].size, 4 * terms[0].size),
        compiler_params=pltpu.CompilerParams(vmem_limit_bytes=2 * MIB),
    )(*terms)


def cost(flops, read):
    return pl.CostEstimate(flops=flops // 1000, bytes_accessed=read // 1000, transcendentals=0)


PART = 256
LANES = 128


def attend(base, len_ref, q_ref, nk_ref, nv_ref, k_buf, v_buf, out_buf, wait):
    steps = q_ref.shape[0]
    count, copies, slots, head = k_buf.shape
    group = q_ref.shape[2] // (copies * head)
    rows = steps * group
    batch = 4
    scaling = head ** (-0.5)
    slot = lax.broadcasted_iota(jnp.int32, (rows, slots), 1)
    step = lax.broadcasted_iota(jnp.int32, (rows, 1), 0) // group
    for b0 in range(0, count, batch):
        seqs = range(b0, min(b0 + batch, count))
        work = [(b, g) for b in seqs for g in range(copies)]
        asked, recent = [], []
        for b, g in work:
            at = base + b
            pick = [
                q_ref[s, at : at + 1, (g * group + j) * head : (g * group + j + 1) * head]
                for s in range(steps)
                for j in range(group)
            ]
            wide = jnp.concatenate([p.astype(F32) for p in pick], axis=0)
            asked.append(wide.astype(BF16))
            found = []
            for r in range(steps):
                key = nk_ref[r, at, g : g + 1, :].astype(F32)
                score = jnp.sum(wide * key, axis=1, keepdims=True) * scaling
                found.append(jnp.where(step >= r, score, -jnp.inf))
            recent.append(found)
        for b in seqs:
            wait(b)
        alive = {
            b: slot < jnp.broadcast_to(len_ref[base + b : base + b + 1, :1], (rows, slots))
            for b in seqs
        }
        scores = [
            lax.dot_general(q, k_buf[b, g], (((1,), (1,)), ((), ())), preferred_element_type=F32)
            for q, (b, g) in zip(asked, work)
        ]
        scores = [
            jnp.where(alive[b], s * scaling, -jnp.inf) for s, (b, g) in zip(scores, work)
        ]
        tops = [
            functools.reduce(jnp.maximum, [jnp.max(s, axis=1, keepdims=True)] + found)
            for s, found in zip(scores, recent)
        ]
        weights = [jnp.exp(s - top) for s, top in zip(scores, tops)]
        fresh = [[jnp.exp(x - top) for x in found] for found, top in zip(recent, tops)]
        totals = [jnp.sum(w, axis=1, keepdims=True) + sum(f) for w, f in zip(weights, fresh)]
        blends = [
            jnp.dot(w.astype(BF16), v_buf[b, g], preferred_element_type=F32)
            for w, (b, g) in zip(weights, work)
        ]
        for (b, g), blend, f, total in zip(work, blends, fresh, totals):
            for r in range(steps):
                value = nv_ref[r, base + b, g : g + 1, :].astype(F32)
                blend = blend + f[r].astype(BF16).astype(F32) * value
            out = blend / total
            for s in range(steps):
                for j in range(group):
                    cols = slice((g * group + j) * head, (g * group + j + 1) * head)
                    at = s * count + b
                    out_buf[at : at + 1, cols] = out[s * group + j : s * group + j + 1, :]


def first_attention(len_hbm, q_hbm, nk_hbm, nv_hbm, k_hbm, v_hbm, *refs):
    o_ref, lens_ref, q_ref, nk_ref, nv_ref, k_next, v_next = refs[:7]
    len_ref, k_buf, v_buf, out_buf, sem, small_sem = refs[7:]
    count, copies, slots, head = k_buf.shape
    ends = ((len_hbm, len_ref), (q_hbm, q_ref), (nk_hbm, nk_ref), (nv_hbm, nv_ref))
    small = [
        pltpu.make_async_copy(src, dst, small_sem.at[k]) for k, (src, dst) in enumerate(ends)
    ]

    def moves(b, c):
        here = pl.ds(c * PART, PART)
        k_to, v_to = (k_buf, v_buf) if b < count else (k_next, v_next)
        return (
            pltpu.make_async_copy(k_hbm.at[b, :, here], k_to.at[b % count, :, here], sem.at[0, b]),
            pltpu.make_async_copy(v_hbm.at[b, :, here], v_to.at[b % count, :, here], sem.at[1, b]),
        )

    def start(b, c):
        for move in moves(b, c):
            move.start()

    def clear(b, c):
        v_to = v_buf if b < count else v_next
        v_to[b % count, :, c * PART : (c + 1) * PART] = jnp.zeros((copies, PART, head), BF16)

    def wait_part(b, c):
        for move in moves(b, c):
            move.wait()

    def wait(b):
        wait_part(b, 0)
        for c in range(1, slots // PART):
            pl.when(len_ref[b] > c * PART)(functools.partial(wait_part, b, c))

    for move in small:
        move.start()
    start(0, 0)
    small[0].wait()
    for b in range(2 * count):
        if b:
            start(b, 0)
        for c in range(1, slots // PART):
            live = len_ref[b] > c * PART
            pl.when(live)(functools.partial(start, b, c))
            pl.when(jnp.logical_not(live))(functools.partial(clear, b, c))
        lens_ref[b : b + 1, :] = jnp.full((1, lens_ref.shape[1]), len_ref[b], jnp.int32)
    for move in small[1:]:
        move.wait()
    attend(0, lens_ref, q_ref, nk_ref, nv_ref, k_buf, v_buf, out_buf, wait)
    o_ref[...] = out_buf[...].astype(BF16)
    for b in range(count, 2 * count):
        wait(b)


def second_attention(lens_ref, q_ref, nk_ref, nv_ref, k_ref, v_ref, o_ref, out_buf):
    none = lambda b: None
    attend(k_ref.shape[0], lens_ref, q_ref, nk_ref, nv_ref, k_ref, v_ref, out_buf, none)
    o_ref[...] = out_buf[...].astype(BF16)


def attention_first(queries, new_keys, new_values, key_cache, value_cache, lengths):
    steps, seqs, deep = queries.shape
    _, copies, slots, head = key_cache.shape
    count = seqs // 2
    vmem = pl.BlockSpec(memory_space=pltpu.VMEM)
    hbm = pl.BlockSpec(memory_space=pl.ANY)
    buffer = pltpu.VMEM((count, copies, slots, head), BF16)
    moved = [lengths, queries, new_keys, new_values, key_cache, value_cache]
    moved = [pltpu.with_memory_space_constraint(x, pltpu.HBM) for x in moved]
    heads, *carried = pl.pallas_call(
        first_attention,
        in_specs=[hbm] * 6,
        out_specs=[vmem] * 7,
        out_shape=[
            pltpu.VMEM((steps * count, deep), BF16),
            pltpu.VMEM((seqs, 128), jnp.int32),
            pltpu.VMEM(queries.shape, BF16),
            pltpu.VMEM(new_keys.shape, BF16),
            pltpu.VMEM(new_values.shape, BF16),
            buffer,
            buffer,
        ],
        scratch_shapes=[
            pltpu.SMEM(lengths.shape, lengths.dtype),
            buffer,
            buffer,
            pltpu.VMEM((steps * count, deep), F32),
            pltpu.SemaphoreType.DMA((2, seqs)),
            pltpu.SemaphoreType.DMA((4,)),
        ],
        cost_estimate=cost(2 * seqs * slots * deep, 8 * count * copies * slots * head),
        compiler_params=pltpu.CompilerParams(vmem_limit_bytes=12 * MIB),
    )(*moved)
    return heads, carried


def attention_second(carried):
    lens, queries, new_keys, new_values, keys, values = carried
    steps, seqs, deep = queries.shape
    count = seqs // 2
    vmem = pl.BlockSpec(memory_space=pltpu.VMEM)
    return pl.pallas_call(
        second_attention,
        in_specs=[vmem] * 6,
        out_specs=vmem,
        out_shape=jax.ShapeDtypeStruct((steps * count, deep), BF16),
        scratch_shapes=[pltpu.VMEM((steps * count, deep), F32)],
        cost_estimate=cost(2 * seqs * keys.shape[2] * deep, 2 * keys.size),
        compiler_params=pltpu.CompilerParams(vmem_limit_bytes=4 * MIB),
    )(*carried)


def fetch_kernel(pieces, where_ref, src_ref, *refs):
    o_refs, sem = refs[-3:-1], refs[-1]
    length = o_refs[0].shape[0]
    step = length // pieces
    moves = []
    for flip, o_ref in enumerate(o_refs):
        for k in range(pieces):
            at = pl.multiple_of((where_ref[1] ^ flip) * length + k * step, 16)
            moves.append(
                pltpu.make_async_copy(
                    src_ref.at[pl.ds(at, step)], o_ref.at[pl.ds(k * step, step)], sem.at[flip, k]
                )
            )
    for move in moves:
        move.start()
    for move in moves:
        move.wait()


def fetch(where, weight, after):
    src = pltpu.with_memory_space_constraint(weight, pltpu.HBM)
    hbm = pl.BlockSpec(memory_space=pl.ANY)
    pieces = 4
    half = pltpu.VMEM((weight.shape[0] // 2, weight.shape[1]), weight.dtype)
    return pl.pallas_call(
        functools.partial(fetch_kernel, pieces),
        in_specs=[pl.BlockSpec(memory_space=pltpu.SMEM)] + [hbm] * (1 + len(after)),
        out_specs=[pl.BlockSpec(memory_space=pltpu.VMEM)] * 2,
        out_shape=[half] * 2,
        scratch_shapes=[pltpu.SemaphoreType.DMA((2, pieces))],
        cost_estimate=cost(0, weight.size),
        compiler_params=pltpu.CompilerParams(vmem_limit_bytes=1 * MIB),
    )(where, src, *after)


def half_of(where_ref, flip, length):
    return pl.ds(pl.multiple_of((where_ref[1] ^ flip) * length, 128), length)


def product_kernel(flips, where_ref, *refs):
    bufs, refs = refs[-1], refs[:-1]
    w_ref, o_refs = refs[-1 - len(flips)], refs[-len(flips) :]
    for n, flip in enumerate(flips):
        count = refs[0].shape[0]
        buf = bufs.at[n]
        for k, block_ref in enumerate(refs[4 * n : 4 * n + 4]):
            at = pl.multiple_of((where_ref[0] ^ k) * count, count)
            buf[pl.ds(at, count), :] = block_ref[...]
        cols = half_of(where_ref, flip, o_refs[n].shape[1])
        out = jnp.dot(buf[...], w_ref[:, cols], preferred_element_type=F32)
        o_refs[n][...] = out.astype(BF16)


def product(where, w, *jobs):
    count, deep = jobs[0][0][0].shape
    wide = w.shape[1] // 2
    blocks = [block for job in jobs for block in job[0]]
    vmem = pl.BlockSpec(memory_space=pltpu.VMEM)
    return pl.pallas_call(
        functools.partial(product_kernel, [flip for _, flip in jobs]),
        in_specs=[pl.BlockSpec(memory_space=pltpu.SMEM)] + [vmem] * (len(blocks) + 1),
        out_specs=[vmem] * len(jobs),
        out_shape=[jax.ShapeDtypeStruct((4 * count, wide), BF16)] * len(jobs),
        scratch_shapes=[pltpu.VMEM((len(jobs), 4 * count, deep), BF16)],
        cost_estimate=cost(8 * count * deep * wide, 2 * deep * wide),
        compiler_params=pltpu.CompilerParams(vmem_limit_bytes=4 * MIB),
    )(where, *blocks, w)


def middle_kernel(flip, groups, where_ref, *refs):
    attn_refs, (res_ref, gain_ref, mid_ref, normed_ref) = refs[:groups], refs[groups : groups + 4]
    steps = res_ref.shape[0]
    rows, wide = mid_ref.shape
    count = rows // (steps * 4)
    some = count // groups
    cols = half_of(where_ref, flip, wide)
    blocks = [
        res_ref[s, d * count : (d + 1) * count, cols].astype(F32)
        for d in range(4)
        for s in range(steps)
    ]
    parts = [block[n * some : (n + 1) * some] for n in range(groups) for block in blocks]
    attn = jnp.concatenate([ref[...].astype(F32) for ref in attn_refs], axis=0)
    mid = (jnp.concatenate(parts, axis=0) + attn).astype(BF16)
    whole = mid.astype(F32)
    mid_ref[...] = mid
    normed_ref[...] = (whole * gain_ref[:1, cols].astype(F32)).astype(BF16)
    for sq_ref in refs[groups + 4 :]:
        sq_ref[...] = jnp.broadcast_to(jnp.sum(whole * whole, axis=1, keepdims=True), sq_ref.shape)


def middle_part(where, flip, attn, residual, gain):
    rows, wide = attn[0].shape[0] * len(attn), attn[0].shape[1]
    vmem = pl.BlockSpec(memory_space=pltpu.VMEM)
    outs = [jax.ShapeDtypeStruct((rows, wide), BF16)] * 2
    outs.append(jax.ShapeDtypeStruct((rows, LANES), F32))
    return pl.pallas_call(
        functools.partial(middle_kernel, flip, len(attn)),
        in_specs=[pl.BlockSpec(memory_space=pltpu.SMEM)] + [vmem] * (len(attn) + 2),
        out_specs=[vmem] * len(outs),
        out_shape=outs,
        cost_estimate=cost(8 * rows * wide, 8 * rows * wide),
        compiler_params=pltpu.CompilerParams(vmem_limit_bytes=6 * MIB),
    )(where, *attn, residual, gain)


def first_kernel(wide, where_ref, x_ref, g_ref, u_ref, o_ref):
    deep, all_rows = half_of(where_ref, 0, x_ref.shape[1]), slice(None)
    length = g_ref.shape[1]
    for k, w_ref in enumerate((g_ref, u_ref)):
        for at in range(0, length, wide):
            here = slice(at, at + wide)
            out = jnp.dot(x_ref[...], w_ref[deep if k else all_rows, here], preferred_element_type=F32)
            o_ref[:, k * length + at : k * length + at + wide] = out


def gate_up_first(where, x, weights):
    rows, deep = x.shape
    length = weights[0].shape[1]
    vmem = pl.BlockSpec(memory_space=pltpu.VMEM)
    return pl.pallas_call(
        functools.partial(first_kernel, length // 7),
        in_specs=[pl.BlockSpec(memory_space=pltpu.SMEM)] + [vmem] * 3,
        out_specs=vmem,
        out_shape=jax.ShapeDtypeStruct((rows, 2 * length), F32),
        cost_estimate=cost(4 * rows * deep * length, 4 * deep * length),
        compiler_params=pltpu.CompilerParams(vmem_limit_bytes=4 * MIB),
    )(where, x, *weights)


def packed(whole):
    high = whole.astype(BF16).astype(F32)
    middle = (whole - high).astype(BF16).astype(F32)
    low = whole - high - middle
    lane = lax.broadcasted_iota(jnp.int32, whole.shape, 1)
    third = LANES // 4
    return jnp.where(lane < third, high, jnp.where(lane < 2 * third, middle, low)).astype(BF16)


def unpacked(ref):
    start = ref.shape[1] - LANES
    parts = [ref[:, start + k * (LANES // 4) :][:, :1].astype(F32) for k in range(3)]
    return parts[0] + parts[1] + parts[2]


def second_kernel(chip, groups, where_ref, x_ref, f_ref, sq_ref, g_ref, u_ref, *refs):
    give_refs, (keep_ref, buf) = refs[:groups], refs[groups:]
    for n, give_ref in enumerate(give_refs):
        some = give_ref.shape[0]
        give_ref[:, keep_ref.shape[1] :] = packed(sq_ref[n * some : (n + 1) * some, :])
    me = where_ref[0]
    deep, all_rows = half_of(where_ref, 1, x_ref.shape[1]), slice(None)
    length = g_ref.shape[1]
    own = length // 4
    rows = give_refs[0].shape[0]
    start = pl.multiple_of(((me // 2) ^ chip) * (2 * own), 128)
    for k, w_ref in enumerate((g_ref, u_ref)):
        out = jnp.dot(x_ref[...], w_ref[deep if k else all_rows, pl.ds(start, 2 * own)], preferred_element_type=F32)
        buf[...] = out + f_ref[:, pl.ds(pl.multiple_of(k * length + start, 128), 2 * own)]
        mine = pl.ds(pl.multiple_of((me % 2) * own, 128), own)
        other = pl.ds(pl.multiple_of((1 - me % 2) * own, 128), own)
        here = slice(k * own, (k + 1) * own)
        keep_ref[:, here] = buf[:, mine]
        for n, give_ref in enumerate(give_refs):
            give_ref[:, here] = buf[n * rows : (n + 1) * rows, other].astype(BF16)


def gate_up_second(where, x, first, sq, weights, chip, groups):
    rows, deep = x.shape
    length = weights[0].shape[1]
    own = length // 4
    vmem = pl.BlockSpec(memory_space=pltpu.VMEM)
    *give, keep = pl.pallas_call(
        functools.partial(second_kernel, chip, groups),
        in_specs=[pl.BlockSpec(memory_space=pltpu.SMEM)] + [vmem] * 5,
        out_specs=[vmem] * (groups + 1),
        out_shape=[jax.ShapeDtypeStruct((rows // groups, 2 * own + LANES), BF16)] * groups
        + [jax.ShapeDtypeStruct((rows, 2 * own), F32)],
        scratch_shapes=[pltpu.VMEM((rows, 2 * own), F32)],
        cost_estimate=cost(4 * rows * deep * 2 * own, 8 * deep * own),
        compiler_params=pltpu.CompilerParams(vmem_limit_bytes=6 * MIB),
    )(where, x, first, sq, *weights)
    return give, keep


def relay_kernel(n, keep_ref, got_ref, sq_ref, o_ref):
    rows, cols = got_ref.shape[0], keep_ref.shape[1]
    here = slice(n * rows, (n + 1) * rows)
    o_ref[:, :cols] = (keep_ref[here, :] + got_ref[:, :cols].astype(F32)).astype(BF16)
    o_ref[:, cols:] = packed(sq_ref[here, :] + unpacked(got_ref))


def relay(n, keep, got, sq):
    vmem = pl.BlockSpec(memory_space=pltpu.VMEM)
    return pl.pallas_call(
        functools.partial(relay_kernel, n),
        in_specs=[vmem] * 3,
        out_specs=vmem,
        out_shape=jax.ShapeDtypeStruct(got.shape, BF16),
        cost_estimate=cost(got.size, 4 * got.size),
        compiler_params=pltpu.CompilerParams(vmem_limit_bytes=2 * MIB),
    )(keep, got, sq)


def act_kernel(n, full, near_ref, got_ref, far_ref, sq_ref, o_ref):
    rows, cols = o_ref.shape
    here = slice(n * rows, (n + 1) * rows)
    total = sq_ref[here, :1] + unpacked(got_ref) + unpacked(far_ref)
    inv_norm = lax.rsqrt(total / full + 1e-05)
    both = near_ref[here, :] + got_ref[:, : 2 * cols].astype(F32)
    both = both + far_ref[:, : 2 * cols].astype(F32)
    gate = both[:, :cols] * inv_norm
    up = both[:, cols:] * inv_norm
    o_ref[...] = (gate / (1.0 + jnp.exp(-gate)) * up).astype(BF16)


def act(n, near, got, far, sq, full):
    rows, both = got.shape[0], near.shape[1]
    vmem = pl.BlockSpec(memory_space=pltpu.VMEM)
    return pl.pallas_call(
        functools.partial(act_kernel, n, full),
        in_specs=[vmem] * 4,
        out_specs=vmem,
        out_shape=jax.ShapeDtypeStruct((rows, both // 2), BF16),
        cost_estimate=cost(8 * rows * both, 8 * rows * both),
        compiler_params=pltpu.CompilerParams(vmem_limit_bytes=4 * MIB),
    )(near, got, far, sq)


def final_kernel(groups, where_ref, *refs):
    mid_refs, ffn_refs, o_ref = refs[:2], refs[2:-1], refs[-1]
    steps = o_ref.shape[0]
    rows, wide = ffn_refs[0].shape
    some = rows // (steps * 4)
    count = some * groups
    for flip in range(2):
        cols = half_of(where_ref, flip, wide)
        outs = [
            mid_refs[flip][n * rows : (n + 1) * rows, :].astype(F32)
            + ffn_refs[2 * n + flip][...].astype(F32)
            for n in range(groups)
        ]
        for d in range(4):
            for s in range(steps):
                at = (d * steps + s) * some
                block = jnp.concatenate([out[at : at + some] for out in outs], axis=0)
                o_ref[s, d * count : (d + 1) * count, cols] = block.astype(BF16)


def final(where, mids, groups, shape):
    vmem = pl.BlockSpec(memory_space=pltpu.VMEM)
    flat = [*mids, *(x for group in groups for x in group)]
    return pl.pallas_call(
        functools.partial(final_kernel, len(groups)),
        in_specs=[pl.BlockSpec(memory_space=pltpu.SMEM)] + [vmem] * len(flat),
        out_specs=vmem,
        out_shape=jax.ShapeDtypeStruct(shape, BF16),
        cost_estimate=cost(2 * shape[1] * shape[2], 8 * shape[1] * shape[2]),
        compiler_params=pltpu.CompilerParams(vmem_limit_bytes=6 * MIB),
    )(where, *flat)


def down_kernel(jobs, where_ref, *refs):
    bufs, refs = refs[-1], refs[:-1]
    ins, w_ref, o_refs = refs[: -1 - len(jobs)], refs[-1 - len(jobs)], refs[-len(jobs) :]
    me = where_ref[0]
    for k, (chip, flip, has_sum) in enumerate(jobs):
        mine_ref, other_ref, *sums = ins[: 2 + has_sum]
        ins = ins[2 + has_sum :]
        own = mine_ref.shape[1]
        buf = bufs.at[k]
        buf[:, pl.ds(pl.multiple_of((me % 2) * own, 128), own)] = mine_ref[...]
        buf[:, pl.ds(pl.multiple_of((1 - me % 2) * own, 128), own)] = other_ref[...]
        at = pl.ds(pl.multiple_of(((me // 2) ^ chip) * (2 * own), 128), 2 * own)
        o_ref = o_refs[k]
        cols = slice(None) if flip is None else half_of(where_ref, flip, o_ref.shape[1])
        total = jnp.dot(buf[...], w_ref[at, cols], preferred_element_type=F32)
        for ref in sums:
            total = total + ref[:, cols]
        o_ref[...] = total.astype(o_ref.dtype)


def down(where, weight, *jobs):
    args, keys, outs = [where], [], []
    for mine, other, chip, flip, total in jobs:
        args += [mine, other] + ([] if total is None else [total])
        keys.append((chip, flip, int(total is not None)))
        wide = weight.shape[1] // (1 if flip is None else 2)
        dtype = F32 if total is None else BF16
        outs.append(jax.ShapeDtypeStruct((mine.shape[0], wide), dtype))
    rows, own = jobs[0][0].shape
    vmem = pl.BlockSpec(memory_space=pltpu.VMEM)
    return pl.pallas_call(
        functools.partial(down_kernel, keys),
        in_specs=[pl.BlockSpec(memory_space=pltpu.SMEM)] + [vmem] * len(args),
        out_specs=[vmem] * len(jobs),
        out_shape=outs,
        scratch_shapes=[pltpu.VMEM((len(jobs), rows, 2 * own), BF16)],
        cost_estimate=cost(4 * rows * own * weight.shape[1], 4 * own * weight.shape[1]),
        compiler_params=pltpu.CompilerParams(vmem_limit_bytes=4 * MIB),
    )(*args, weight)


def pairs(size, step):
    return [(i, i ^ step) for i in range(size)]


def in_order(mine, other, bit, axis=0):
    first = jnp.where(bit == 0, mine, other)
    second = jnp.where(bit == 0, other, mine)
    return jnp.concatenate((first, second), axis=axis)


def levels(size):
    return [1 << k for k in range(size.bit_length() - 1)]


def gather_rows(block, size):
    me = lax.axis_index("dp")
    count, deep = block.shape
    for step in reversed(levels(size)):
        bit = (me // step) % 2
        block = in_order(block, lax.ppermute(block, "dp", pairs(size, step)), bit)
    block = block.reshape(size, count, deep)
    order = []
    for d in range(size):
        place = 0
        for step in levels(size):
            place = place * 2 + (d // step) % 2
        order.append(block[place])
    return jnp.concatenate(order, axis=0)


def sum_dp(value, size):
    for step in levels(size):
        value = value + lax.ppermute(value, "dp", pairs(size, step))
    return value


def activate(both, inv_norm):
    cols = both.shape[1] // 2
    gate = both[:, :cols] * inv_norm
    up = both[:, cols:] * inv_norm
    return (jax.nn.silu(gate) * up).astype(BF16)


def middle(resid, attn, norm_gain, dp):
    mid = add(resid, attn)
    wide = mid.astype(F32)
    squares = sum_dp(jnp.sum(wide * wide, axis=1)[None, :], dp)
    inv_norm = lax.rsqrt(squares / (mid.shape[1] * dp) + 1e-05).reshape(mid.shape[0], 1)
    normed = (wide * norm_gain.astype(F32)[None, :]).astype(BF16)
    return mid, inv_norm, normed


def plain(rows, resid, out_weight, norm_gain, gate_weight, up_weight, down_weight, dp):
    part = jnp.dot(rows, out_weight, preferred_element_type=F32).astype(BF16)
    mid, inv_norm, normed = middle(resid, lax.psum(part, "tensor"), norm_gain, dp)
    both = []
    for weight in (gate_weight, up_weight):
        term = jnp.dot(normed, weight, preferred_element_type=F32).astype(BF16)
        both.append(lax.psum_scatter(term, "dp", scatter_dimension=1, tiled=True).astype(F32))
    hidden = activate(jnp.concatenate(both, axis=1), inv_norm)
    hidden = lax.all_gather(hidden, "dp", axis=1, tiled=True)
    part = jnp.dot(hidden, down_weight, preferred_element_type=F32).astype(BF16)
    return add(mid, lax.psum(part, "tensor"))


def body(
    residual,
    queries,
    new_keys,
    new_values,
    key_cache,
    value_cache,
    lengths,
    out_weight,
    norm_gain,
    gate_weight,
    up_weight,
    down_weight,
):
    dp = lax.axis_size("dp")
    tensor = lax.axis_size("tensor")
    steps, all_seqs, width = residual.shape
    local_seqs = queries.shape[1]
    where = jnp.stack([lax.axis_index("dp"), lax.axis_index("tensor") % 2])
    where, queries = lax.optimization_barrier((where, queries))
    heads, carried = attention_first(
        queries, new_keys, new_values, key_cache, value_cache, lengths
    )
    if dp == 4 and tensor == 4:
        weights = out_weight, gate_weight, up_weight, down_weight
        gain, heads = lax.optimization_barrier((norm_gain, heads))
        return fast(where, heads, carried, residual, gain, *weights)
    heads = jnp.stack((heads, attention_second(carried)))
    heads = heads.reshape(2, steps, local_seqs // 2, -1).swapaxes(0, 1)
    heads = heads.reshape(steps * local_seqs, -1)
    row_count = steps * all_seqs
    resid = residual.reshape(steps, dp, local_seqs, width).swapaxes(0, 1)
    weights = out_weight, norm_gain, gate_weight, up_weight, down_weight
    out = plain(gather_rows(heads, dp), resid.reshape(row_count, width), *weights, dp)
    return out.reshape(dp, steps, local_seqs, width).swapaxes(0, 1).reshape(residual.shape)


def fast(where, heads, carried, residual, gain, out_w, gate_weight, up_weight, down_weight):
    width = out_w.shape[1]
    groups = 2
    core = lambda value: lax.ppermute(value, "dp", pairs(4, 1))
    across = lambda value: lax.ppermute(value, "dp", pairs(4, 2))
    swap = lambda value: lax.ppermute(value, "tensor", pairs(4, 1))
    gain = jnp.broadcast_to(gain[None, :], (16, width))
    after = lambda value, *others: lax.optimization_barrier((value, *others))[0]

    def sum_tensor(sends, keeps, during=lambda n, held: None):
        gots = [swap(send) for send in sends]
        helds, crosses = [None, None], [None, None]
        for n in range(2):
            if n:
                gots[n] = after(gots[n], helds[0])
            keep, gots[n] = keeps(n, helds[0], gots[n])
            helds[n] = total_of(keep, gots[n])
            crosses[n] = lax.ppermute(helds[n], "tensor", pairs(4, 2))
        others = [None, None]
        for n in range(2):
            beside = during(n, helds[1 - n])
            if beside is not None:
                crosses[n] = after(crosses[n], beside)
            helds[n] = total_of(helds[n], crosses[n])
            others[n] = swap(helds[n])
            if n == 0:
                crosses[1] = after(crosses[1], helds[0])
        return helds, others

    out_w, up_w, down_w = [
        pltpu.with_memory_space_constraint(w, pltpu.VMEM) for w in (out_w, up_weight, down_weight)
    ]
    far_a = across(heads)
    heads_b = attention_second(carried)
    far_a, heads_b = lax.optimization_barrier((far_a, heads_b))
    far_b = across(heads_b)
    blocks_a = [heads, core(heads), far_a, core(far_a)]
    blocks_a, gain = lax.optimization_barrier((blocks_a, gain))
    (send_a,) = product(where, out_w, (blocks_a, 1))
    far_b, send_a = lax.optimization_barrier((far_b, send_a))
    blocks_b = [heads_b, core(heads_b), far_b, core(far_b)]
    keep_a, send_b = product(where, out_w, (blocks_a, 0), (blocks_b, 1))
    gate = []

    def keeps(n, held, got):
        if n == 0:
            return keep_a, got
        return product(where, out_w, (after(blocks_b, held), 0))[0], got

    def during(n, held):
        if n == 0:
            gate.extend(fetch(where, gate_weight, [held]))
            return gate[1]

    helds, others = sum_tensor([send_a, send_b], keeps, during)
    mid, normed, sq = middle_part(where, 0, helds, residual, gain)
    first = gate_up_first(where, normed, (gate[0], up_w))
    others, first = lax.optimization_barrier((others, first))
    mid_other, normed, sq_other = middle_part(where, 1, others, residual, gain)
    sq = total_of(sq, sq_other, dtype=F32)
    weights = gate[1], up_w
    give, keep = gate_up_second(where, normed, first, sq, weights, 1, groups)
    far = [core(x) for x in give]
    relayed = [relay(n, keep, x, sq) for n, x in enumerate(far)]
    far = [across(x) for x in relayed]
    normed, relayed = lax.optimization_barrier((normed, relayed))
    give, near = gate_up_second(where, normed, first, sq, weights, 0, groups)
    got = [core(x) for x in give]
    far[0], near, got = lax.optimization_barrier((far[0], near, got))

    def activated(n):
        mine = act(n, near, got[n], far[n], sq, width * 4)
        other = core(mine)
        return mine, across(mine), other

    def early(n):
        return down(where, down_w, (mine[n], other[n], 0, None, None))[0]

    def last(n, flip, total):
        return mine_far[n], other_far[n], 1, flip, total

    mine, mine_far, other, totals, other_far = [0] * 2, [0] * 2, [0] * 2, [0] * 2, [0] * 2
    mine[0], mine_far[0], other[0] = activated(0)
    totals[0] = early(0)
    far[1] = after(far[1], totals[0])
    mine[1], mine_far[1], other[1] = activated(1)
    mine_far[0] = after(mine_far[0], mine[1])
    other_far[0] = core(mine_far[0])
    totals[1] = early(1)
    other_far[0] = after(other_far[0], totals[1])
    (send_a,) = down(where, down_w, last(0, 1, totals[0]))
    mine_far[1] = after(mine_far[1], send_a)
    other_far[1] = core(mine_far[1])
    keep_a, send_b = down(where, down_w, last(0, 0, totals[0]), last(1, 1, totals[1]))

    def keeps(n, held, got):
        if n == 0:
            return keep_a, got
        return down(where, down_w, last(1, 0, after(totals[1], held)))[0], got

    helds, others = sum_tensor([send_a, send_b], keeps)
    outs = list(zip(helds, others))
    return final(where, [mid, mid_other], outs, residual.shape)


def solution(mesh):
    in_specs = (
        P(None, "replica", "dp"),
        P(None, ("replica", "dp"), "tensor"),
        P(None, ("replica", "dp"), "tensor", None),
        P(None, ("replica", "dp"), "tensor", None),
        P(("replica", "dp"), "tensor", None, None),
        P(("replica", "dp"), "tensor", None, None),
        P(("replica", "dp")),
        P("tensor", "dp"),
        P("dp"),
        P("dp", "tensor"),
        P("dp", "tensor"),
        P("tensor", "dp"),
    )
    out_specs = P(None, "replica", "dp")
    return jax.shard_map(body, mesh=mesh, in_specs=in_specs, out_specs=out_specs, check_vma=False)
```

```python
import functools

import jax
import jax.numpy as jnp
from jax import lax
from jax.experimental import pallas as pl
from jax.experimental.pallas import tpu as pltpu
from jax.sharding import PartitionSpec as P

BF16 = jnp.bfloat16
F32 = jnp.float32
MIB = 1 << 20


def add(a, b):
    return (a.astype(F32) + b.astype(F32)).astype(BF16)


def sum_kernel(dtype, *refs):
    total = functools.reduce(jnp.add, [ref[...].astype(F32) for ref in refs[:-1]])
    refs[-1][...] = total.astype(dtype)


def total_of(*terms, dtype=BF16):
    vmem = pl.BlockSpec(memory_space=pltpu.VMEM)
    return pl.pallas_call(
        functools.partial(sum_kernel, dtype),
        in_specs=[vmem] * len(terms),
        out_specs=vmem,
        out_shape=jax.ShapeDtypeStruct(terms[0].shape, dtype),
        cost_estimate=cost(terms[0].size, 4 * terms[0].size),
        compiler_params=pltpu.CompilerParams(vmem_limit_bytes=2 * MIB),
    )(*terms)


def cost(flops, read):
    return pl.CostEstimate(flops=flops // 1000, bytes_accessed=read // 1000, transcendentals=0)


PART = 256
LANES = 128


def attend(base, len_ref, q_ref, nk_ref, nv_ref, k_buf, v_buf, out_buf, wait):
    steps = q_ref.shape[0]
    count, copies, slots, head = k_buf.shape
    group = q_ref.shape[2] // (copies * head)
    rows = steps * group
    batch = 4
    scaling = head ** (-0.5)
    slot = lax.broadcasted_iota(jnp.int32, (rows, slots), 1)
    step = lax.broadcasted_iota(jnp.int32, (rows, 1), 0) // group
    for b0 in range(0, count, batch):
        seqs = range(b0, min(b0 + batch, count))
        work = [(b, g) for b in seqs for g in range(copies)]
        asked, recent = [], []
        for b, g in work:
            at = base + b
            pick = [
                q_ref[s, at : at + 1, (g * group + j) * head : (g * group + j + 1) * head]
                for s in range(steps)
                for j in range(group)
            ]
            wide = jnp.concatenate([p.astype(F32) for p in pick], axis=0)
            asked.append(wide.astype(BF16))
            found = []
            for r in range(steps):
                key = nk_ref[r, at, g : g + 1, :].astype(F32)
                score = jnp.sum(wide * key, axis=1, keepdims=True) * scaling
                found.append(jnp.where(step >= r, score, -jnp.inf))
            recent.append(found)
        for b in seqs:
            wait(b)
        alive = {
            b: slot < jnp.broadcast_to(len_ref[base + b : base + b + 1, :1], (rows, slots))
            for b in seqs
        }
        scores = [
            lax.dot_general(q, k_buf[b, g], (((1,), (1,)), ((), ())), preferred_element_type=F32)
            for q, (b, g) in zip(asked, work)
        ]
        scores = [
            jnp.where(alive[b], s * scaling, -jnp.inf) for s, (b, g) in zip(scores, work)
        ]
        tops = [
            functools.reduce(jnp.maximum, [jnp.max(s, axis=1, keepdims=True)] + found)
            for s, found in zip(scores, recent)
        ]
        weights = [jnp.exp(s - top) for s, top in zip(scores, tops)]
        fresh = [[jnp.exp(x - top) for x in found] for found, top in zip(recent, tops)]
        totals = [jnp.sum(w, axis=1, keepdims=True) + sum(f) for w, f in zip(weights, fresh)]
        blends = [
            jnp.dot(w.astype(BF16), v_buf[b, g], preferred_element_type=F32)
            for w, (b, g) in zip(weights, work)
        ]
        for (b, g), blend, f, total in zip(work, blends, fresh, totals):
            for r in range(steps):
                value = nv_ref[r, base + b, g : g + 1, :].astype(F32)
                blend = blend + f[r].astype(BF16).astype(F32) * value
            out = blend / total
            for s in range(steps):
                for j in range(group):
                    cols = slice((g * group + j) * head, (g * group + j + 1) * head)
                    at = s * count + b
                    out_buf[at : at + 1, cols] = out[s * group + j : s * group + j + 1, :]


def first_attention(len_hbm, q_hbm, nk_hbm, nv_hbm, k_hbm, v_hbm, *refs):
    o_ref, lens_ref, q_ref, nk_ref, nv_ref, k_next, v_next = refs[:7]
    len_ref, k_buf, v_buf, out_buf, sem, small_sem = refs[7:]
    count, copies, slots, head = k_buf.shape
    ends = ((len_hbm, len_ref), (q_hbm, q_ref), (nk_hbm, nk_ref), (nv_hbm, nv_ref))
    small = [
        pltpu.make_async_copy(src, dst, small_sem.at[k]) for k, (src, dst) in enumerate(ends)
    ]

    def moves(b, c):
        here = pl.ds(c * PART, PART)
        k_to, v_to = (k_buf, v_buf) if b < count else (k_next, v_next)
        return (
            pltpu.make_async_copy(k_hbm.at[b, :, here], k_to.at[b % count, :, here], sem.at[0, b]),
            pltpu.make_async_copy(v_hbm.at[b, :, here], v_to.at[b % count, :, here], sem.at[1, b]),
        )

    def start(b, c):
        for move in moves(b, c):
            move.start()

    def clear(b, c):
        v_to = v_buf if b < count else v_next
        v_to[b % count, :, c * PART : (c + 1) * PART] = jnp.zeros((copies, PART, head), BF16)

    def wait_part(b, c):
        for move in moves(b, c):
            move.wait()

    def wait(b):
        wait_part(b, 0)
        for c in range(1, slots // PART):
            pl.when(len_ref[b] > c * PART)(functools.partial(wait_part, b, c))

    for move in small:
        move.start()
    for b in range(count):
        start(b, 0)
    small[0].wait()
    for b in range(2 * count):
        if b >= count:
            start(b, 0)
        for c in range(1, slots // PART):
            live = len_ref[b] > c * PART
            pl.when(live)(functools.partial(start, b, c))
            pl.when(jnp.logical_not(live))(functools.partial(clear, b, c))
        lens_ref[b : b + 1, :] = jnp.full((1, lens_ref.shape[1]), len_ref[b], jnp.int32)
    for move in small[1:]:
        move.wait()
    attend(0, lens_ref, q_ref, nk_ref, nv_ref, k_buf, v_buf, out_buf, wait)
    o_ref[...] = out_buf[...].astype(BF16)
    for b in range(count, 2 * count):
        wait(b)


def second_attention(lens_ref, q_ref, nk_ref, nv_ref, k_ref, v_ref, o_ref, out_buf):
    none = lambda b: None
    attend(k_ref.shape[0], lens_ref, q_ref, nk_ref, nv_ref, k_ref, v_ref, out_buf, none)
    o_ref[...] = out_buf[...].astype(BF16)


def attention_first(queries, new_keys, new_values, key_cache, value_cache, lengths):
    steps, seqs, deep = queries.shape
    _, copies, slots, head = key_cache.shape
    count = seqs // 2
    vmem = pl.BlockSpec(memory_space=pltpu.VMEM)
    hbm = pl.BlockSpec(memory_space=pl.ANY)
    buffer = pltpu.VMEM((count, copies, slots, head), BF16)
    moved = [lengths, queries, new_keys, new_values, key_cache, value_cache]
    moved = [pltpu.with_memory_space_constraint(x, pltpu.HBM) for x in moved]
    heads, *carried = pl.pallas_call(
        first_attention,
        in_specs=[hbm] * 6,
        out_specs=[vmem] * 7,
        out_shape=[
            pltpu.VMEM((steps * count, deep), BF16),
            pltpu.VMEM((seqs, 128), jnp.int32),
            pltpu.VMEM(queries.shape, BF16),
            pltpu.VMEM(new_keys.shape, BF16),
            pltpu.VMEM(new_values.shape, BF16),
            buffer,
            buffer,
        ],
        scratch_shapes=[
            pltpu.SMEM(lengths.shape, lengths.dtype),
            buffer,
            buffer,
            pltpu.VMEM((steps * count, deep), F32),
            pltpu.SemaphoreType.DMA((2, seqs)),
            pltpu.SemaphoreType.DMA((4,)),
        ],
        cost_estimate=cost(2 * seqs * slots * deep, 8 * count * copies * slots * head),
        compiler_params=pltpu.CompilerParams(vmem_limit_bytes=12 * MIB),
    )(*moved)
    return heads, carried


def attention_second(carried):
    lens, queries, new_keys, new_values, keys, values = carried
    steps, seqs, deep = queries.shape
    count = seqs // 2
    vmem = pl.BlockSpec(memory_space=pltpu.VMEM)
    return pl.pallas_call(
        second_attention,
        in_specs=[vmem] * 6,
        out_specs=vmem,
        out_shape=jax.ShapeDtypeStruct((steps * count, deep), BF16),
        scratch_shapes=[pltpu.VMEM((steps * count, deep), F32)],
        cost_estimate=cost(2 * seqs * keys.shape[2] * deep, 2 * keys.size),
        compiler_params=pltpu.CompilerParams(vmem_limit_bytes=4 * MIB),
    )(*carried)


def fetch_kernel(pieces, where_ref, src_ref, *refs):
    o_refs, sem = refs[-3:-1], refs[-1]
    length = o_refs[0].shape[0]
    step = length // pieces
    moves = []
    for flip, o_ref in enumerate(o_refs):
        for k in range(pieces):
            at = pl.multiple_of((where_ref[1] ^ flip) * length + k * step, 16)
            moves.append(
                pltpu.make_async_copy(
                    src_ref.at[pl.ds(at, step)], o_ref.at[pl.ds(k * step, step)], sem.at[flip, k]
                )
            )
    for move in moves:
        move.start()
    for move in moves:
        move.wait()


def fetch(where, weight, after):
    src = pltpu.with_memory_space_constraint(weight, pltpu.HBM)
    hbm = pl.BlockSpec(memory_space=pl.ANY)
    pieces = 4
    half = pltpu.VMEM((weight.shape[0] // 2, weight.shape[1]), weight.dtype)
    return pl.pallas_call(
        functools.partial(fetch_kernel, pieces),
        in_specs=[pl.BlockSpec(memory_space=pltpu.SMEM)] + [hbm] * (1 + len(after)),
        out_specs=[pl.BlockSpec(memory_space=pltpu.VMEM)] * 2,
        out_shape=[half] * 2,
        scratch_shapes=[pltpu.SemaphoreType.DMA((2, pieces))],
        cost_estimate=cost(0, weight.size),
        compiler_params=pltpu.CompilerParams(vmem_limit_bytes=1 * MIB),
    )(where, src, *after)


def half_of(where_ref, flip, length):
    return pl.ds(pl.multiple_of((where_ref[1] ^ flip) * length, 128), length)


def product_kernel(flips, where_ref, *refs):
    bufs, refs = refs[-1], refs[:-1]
    w_ref, o_refs = refs[-1 - len(flips)], refs[-len(flips) :]
    for n, flip in enumerate(flips):
        count = refs[0].shape[0]
        buf = bufs.at[n]
        for k, block_ref in enumerate(refs[4 * n : 4 * n + 4]):
            at = pl.multiple_of((where_ref[0] ^ k) * count, count)
            buf[pl.ds(at, count), :] = block_ref[...]
        cols = half_of(where_ref, flip, o_refs[n].shape[1])
        out = jnp.dot(buf[...], w_ref[:, cols], preferred_element_type=F32)
        o_refs[n][...] = out.astype(BF16)


def product(where, w, *jobs):
    count, deep = jobs[0][0][0].shape
    wide = w.shape[1] // 2
    blocks = [block for job in jobs for block in job[0]]
    vmem = pl.BlockSpec(memory_space=pltpu.VMEM)
    return pl.pallas_call(
        functools.partial(product_kernel, [flip for _, flip in jobs]),
        in_specs=[pl.BlockSpec(memory_space=pltpu.SMEM)] + [vmem] * (len(blocks) + 1),
        out_specs=[vmem] * len(jobs),
        out_shape=[jax.ShapeDtypeStruct((4 * count, wide), BF16)] * len(jobs),
        scratch_shapes=[pltpu.VMEM((len(jobs), 4 * count, deep), BF16)],
        cost_estimate=cost(8 * count * deep * wide, 2 * deep * wide),
        compiler_params=pltpu.CompilerParams(vmem_limit_bytes=4 * MIB),
    )(where, *blocks, w)


def middle_kernel(flip, groups, where_ref, *refs):
    attn_refs, (res_ref, gain_ref, mid_ref, normed_ref) = refs[:groups], refs[groups : groups + 4]
    steps = res_ref.shape[0]
    rows, wide = mid_ref.shape
    count = rows // (steps * 4)
    some = count // groups
    cols = half_of(where_ref, flip, wide)
    blocks = [
        res_ref[s, d * count : (d + 1) * count, cols].astype(F32)
        for d in range(4)
        for s in range(steps)
    ]
    parts = [block[n * some : (n + 1) * some] for n in range(groups) for block in blocks]
    attn = jnp.concatenate([ref[...].astype(F32) for ref in attn_refs], axis=0)
    mid = (jnp.concatenate(parts, axis=0) + attn).astype(BF16)
    whole = mid.astype(F32)
    mid_ref[...] = mid
    normed_ref[...] = (whole * gain_ref[:1, cols].astype(F32)).astype(BF16)
    for sq_ref in refs[groups + 4 :]:
        sq_ref[...] = jnp.broadcast_to(jnp.sum(whole * whole, axis=1, keepdims=True), sq_ref.shape)


def middle_part(where, flip, attn, residual, gain):
    rows, wide = attn[0].shape[0] * len(attn), attn[0].shape[1]
    vmem = pl.BlockSpec(memory_space=pltpu.VMEM)
    outs = [jax.ShapeDtypeStruct((rows, wide), BF16)] * 2
    outs.append(jax.ShapeDtypeStruct((rows, LANES), F32))
    return pl.pallas_call(
        functools.partial(middle_kernel, flip, len(attn)),
        in_specs=[pl.BlockSpec(memory_space=pltpu.SMEM)] + [vmem] * (len(attn) + 2),
        out_specs=[vmem] * len(outs),
        out_shape=outs,
        cost_estimate=cost(8 * rows * wide, 8 * rows * wide),
        compiler_params=pltpu.CompilerParams(vmem_limit_bytes=6 * MIB),
    )(where, *attn, residual, gain)


def first_kernel(wide, where_ref, x_ref, g_ref, u_ref, o_ref):
    deep, all_rows = half_of(where_ref, 0, x_ref.shape[1]), slice(None)
    length = g_ref.shape[1]
    for k, w_ref in enumerate((g_ref, u_ref)):
        for at in range(0, length, wide):
            here = slice(at, at + wide)
            out = jnp.dot(x_ref[...], w_ref[deep if k else all_rows, here], preferred_element_type=F32)
            o_ref[:, k * length + at : k * length + at + wide] = out


def gate_up_first(where, x, weights):
    rows, deep = x.shape
    length = weights[0].shape[1]
    vmem = pl.BlockSpec(memory_space=pltpu.VMEM)
    return pl.pallas_call(
        functools.partial(first_kernel, length // 7),
        in_specs=[pl.BlockSpec(memory_space=pltpu.SMEM)] + [vmem] * 3,
        out_specs=vmem,
        out_shape=jax.ShapeDtypeStruct((rows, 2 * length), F32),
        cost_estimate=cost(4 * rows * deep * length, 4 * deep * length),
        compiler_params=pltpu.CompilerParams(vmem_limit_bytes=4 * MIB),
    )(where, x, *weights)


def packed(whole):
    high = whole.astype(BF16).astype(F32)
    middle = (whole - high).astype(BF16).astype(F32)
    low = whole - high - middle
    lane = lax.broadcasted_iota(jnp.int32, whole.shape, 1)
    third = LANES // 4
    return jnp.where(lane < third, high, jnp.where(lane < 2 * third, middle, low)).astype(BF16)


def unpacked(ref):
    start = ref.shape[1] - LANES
    parts = [ref[:, start + k * (LANES // 4) :][:, :1].astype(F32) for k in range(3)]
    return parts[0] + parts[1] + parts[2]


def second_kernel(chip, groups, where_ref, x_ref, f_ref, sq_ref, g_ref, u_ref, *refs):
    give_refs, keep_ref = refs[:groups], refs[groups]
    for n, give_ref in enumerate(give_refs):
        some = give_ref.shape[0]
        give_ref[:, keep_ref.shape[1] :] = packed(sq_ref[n * some : (n + 1) * some, :])
    me = where_ref[0]
    deep, all_rows = half_of(where_ref, 1, x_ref.shape[1]), slice(None)
    length = g_ref.shape[1]
    own = length // 4
    rows = give_refs[0].shape[0]
    start = pl.multiple_of(((me // 2) ^ chip) * (2 * own), 128)
    for k, w_ref in enumerate((g_ref, u_ref)):
        out = jnp.dot(x_ref[...], w_ref[deep if k else all_rows, pl.ds(start, 2 * own)], preferred_element_type=F32)
        out = out + f_ref[:, pl.ds(pl.multiple_of(k * length + start, 128), 2 * own)]
        mine = jnp.where(me % 2 == 0, out[:, :own], out[:, own:])
        other = jnp.where(me % 2 == 0, out[:, own:], out[:, :own]).astype(BF16)
        here = slice(k * own, (k + 1) * own)
        keep_ref[:, here] = mine
        for n, give_ref in enumerate(give_refs):
            give_ref[:, here] = other[n * rows : (n + 1) * rows]


def gate_up_second(where, x, first, sq, weights, chip, groups):
    rows, deep = x.shape
    length = weights[0].shape[1]
    own = length // 4
    vmem = pl.BlockSpec(memory_space=pltpu.VMEM)
    *give, keep = pl.pallas_call(
        functools.partial(second_kernel, chip, groups),
        in_specs=[pl.BlockSpec(memory_space=pltpu.SMEM)] + [vmem] * 5,
        out_specs=[vmem] * (groups + 1),
        out_shape=[jax.ShapeDtypeStruct((rows // groups, 2 * own + LANES), BF16)] * groups
        + [jax.ShapeDtypeStruct((rows, 2 * own), F32)],
        cost_estimate=cost(4 * rows * deep * 2 * own, 8 * deep * own),
        compiler_params=pltpu.CompilerParams(vmem_limit_bytes=6 * MIB),
    )(where, x, first, sq, *weights)
    return give, keep


def relay_kernel(n, keep_ref, got_ref, sq_ref, o_ref):
    rows, cols = got_ref.shape[0], keep_ref.shape[1]
    here = slice(n * rows, (n + 1) * rows)
    o_ref[:, :cols] = (keep_ref[here, :] + got_ref[:, :cols].astype(F32)).astype(BF16)
    o_ref[:, cols:] = packed(sq_ref[here, :] + unpacked(got_ref))


def relay(n, keep, got, sq):
    vmem = pl.BlockSpec(memory_space=pltpu.VMEM)
    return pl.pallas_call(
        functools.partial(relay_kernel, n),
        in_specs=[vmem] * 3,
        out_specs=vmem,
        out_shape=jax.ShapeDtypeStruct(got.shape, BF16),
        cost_estimate=cost(got.size, 4 * got.size),
        compiler_params=pltpu.CompilerParams(vmem_limit_bytes=2 * MIB),
    )(keep, got, sq)


def act_kernel(n, full, near_ref, got_ref, far_ref, sq_ref, o_ref):
    rows, cols = o_ref.shape
    here = slice(n * rows, (n + 1) * rows)
    total = sq_ref[here, :1] + unpacked(got_ref) + unpacked(far_ref)
    inv_norm = lax.rsqrt(total / full + 1e-05)
    both = near_ref[here, :] + got_ref[:, : 2 * cols].astype(F32)
    both = both + far_ref[:, : 2 * cols].astype(F32)
    gate = both[:, :cols] * inv_norm
    up = both[:, cols:] * inv_norm
    o_ref[...] = (gate / (1.0 + jnp.exp(-gate)) * up).astype(BF16)


def act(n, near, got, far, sq, full):
    rows, both = got.shape[0], near.shape[1]
    vmem = pl.BlockSpec(memory_space=pltpu.VMEM)
    return pl.pallas_call(
        functools.partial(act_kernel, n, full),
        in_specs=[vmem] * 4,
        out_specs=vmem,
        out_shape=jax.ShapeDtypeStruct((rows, both // 2), BF16),
        cost_estimate=cost(8 * rows * both, 8 * rows * both),
        compiler_params=pltpu.CompilerParams(vmem_limit_bytes=4 * MIB),
    )(near, got, far, sq)


def final_kernel(groups, where_ref, *refs):
    mid_refs, ffn_refs, o_ref = refs[:2], refs[2:-1], refs[-1]
    steps = o_ref.shape[0]
    rows, wide = ffn_refs[0].shape
    some = rows // (steps * 4)
    count = some * groups
    for flip in range(2):
        cols = half_of(where_ref, flip, wide)
        outs = [
            mid_refs[flip][n * rows : (n + 1) * rows, :].astype(F32)
            + ffn_refs[2 * n + flip][...].astype(F32)
            for n in range(groups)
        ]
        for d in range(4):
            for s in range(steps):
                at = (d * steps + s) * some
                block = jnp.concatenate([out[at : at + some] for out in outs], axis=0)
                o_ref[s, d * count : (d + 1) * count, cols] = block.astype(BF16)


def final(where, mids, groups, shape):
    vmem = pl.BlockSpec(memory_space=pltpu.VMEM)
    flat = [*mids, *(x for group in groups for x in group)]
    return pl.pallas_call(
        functools.partial(final_kernel, len(groups)),
        in_specs=[pl.BlockSpec(memory_space=pltpu.SMEM)] + [vmem] * len(flat),
        out_specs=vmem,
        out_shape=jax.ShapeDtypeStruct(shape, BF16),
        cost_estimate=cost(2 * shape[1] * shape[2], 8 * shape[1] * shape[2]),
        compiler_params=pltpu.CompilerParams(vmem_limit_bytes=6 * MIB),
    )(where, *flat)


def down_kernel(jobs, where_ref, *refs):
    bufs, refs = refs[-1], refs[:-1]
    ins, w_ref, o_refs = refs[: -1 - len(jobs)], refs[-1 - len(jobs)], refs[-len(jobs) :]
    me = where_ref[0]
    for k, (chip, flip, has_sum) in enumerate(jobs):
        mine_ref, other_ref, *sums = ins[: 2 + has_sum]
        ins = ins[2 + has_sum :]
        own = mine_ref.shape[1]
        buf = bufs.at[k]
        buf[:, pl.ds(pl.multiple_of((me % 2) * own, 128), own)] = mine_ref[...]
        buf[:, pl.ds(pl.multiple_of((1 - me % 2) * own, 128), own)] = other_ref[...]
        at = pl.ds(pl.multiple_of(((me // 2) ^ chip) * (2 * own), 128), 2 * own)
        o_ref = o_refs[k]
        cols = slice(None) if flip is None else half_of(where_ref, flip, o_ref.shape[1])
        total = jnp.dot(buf[...], w_ref[at, cols], preferred_element_type=F32)
        for ref in sums:
            total = total + ref[:, cols]
        o_ref[...] = total.astype(o_ref.dtype)


def down(where, weight, *jobs):
    args, keys, outs = [where], [], []
    for mine, other, chip, flip, total in jobs:
        args += [mine, other] + ([] if total is None else [total])
        keys.append((chip, flip, int(total is not None)))
        wide = weight.shape[1] // (1 if flip is None else 2)
        dtype = F32 if total is None else BF16
        outs.append(jax.ShapeDtypeStruct((mine.shape[0], wide), dtype))
    rows, own = jobs[0][0].shape
    vmem = pl.BlockSpec(memory_space=pltpu.VMEM)
    return pl.pallas_call(
        functools.partial(down_kernel, keys),
        in_specs=[pl.BlockSpec(memory_space=pltpu.SMEM)] + [vmem] * len(args),
        out_specs=[vmem] * len(jobs),
        out_shape=outs,
        scratch_shapes=[pltpu.VMEM((len(jobs), rows, 2 * own), BF16)],
        cost_estimate=cost(4 * rows * own * weight.shape[1], 4 * own * weight.shape[1]),
        compiler_params=pltpu.CompilerParams(vmem_limit_bytes=4 * MIB),
    )(*args, weight)


def pairs(size, step):
    return [(i, i ^ step) for i in range(size)]


def in_order(mine, other, bit, axis=0):
    first = jnp.where(bit == 0, mine, other)
    second = jnp.where(bit == 0, other, mine)
    return jnp.concatenate((first, second), axis=axis)


def levels(size):
    return [1 << k for k in range(size.bit_length() - 1)]


def gather_rows(block, size):
    me = lax.axis_index("dp")
    count, deep = block.shape
    for step in reversed(levels(size)):
        bit = (me // step) % 2
        block = in_order(block, lax.ppermute(block, "dp", pairs(size, step)), bit)
    block = block.reshape(size, count, deep)
    order = []
    for d in range(size):
        place = 0
        for step in levels(size):
            place = place * 2 + (d // step) % 2
        order.append(block[place])
    return jnp.concatenate(order, axis=0)


def sum_dp(value, size):
    for step in levels(size):
        value = value + lax.ppermute(value, "dp", pairs(size, step))
    return value


def activate(both, inv_norm):
    cols = both.shape[1] // 2
    gate = both[:, :cols] * inv_norm
    up = both[:, cols:] * inv_norm
    return (jax.nn.silu(gate) * up).astype(BF16)


def middle(resid, attn, norm_gain, dp):
    mid = add(resid, attn)
    wide = mid.astype(F32)
    squares = sum_dp(jnp.sum(wide * wide, axis=1)[None, :], dp)
    inv_norm = lax.rsqrt(squares / (mid.shape[1] * dp) + 1e-05).reshape(mid.shape[0], 1)
    normed = (wide * norm_gain.astype(F32)[None, :]).astype(BF16)
    return mid, inv_norm, normed


def plain(rows, resid, out_weight, norm_gain, gate_weight, up_weight, down_weight, dp):
    part = jnp.dot(rows, out_weight, preferred_element_type=F32).astype(BF16)
    mid, inv_norm, normed = middle(resid, lax.psum(part, "tensor"), norm_gain, dp)
    both = []
    for weight in (gate_weight, up_weight):
        term = jnp.dot(normed, weight, preferred_element_type=F32).astype(BF16)
        both.append(lax.psum_scatter(term, "dp", scatter_dimension=1, tiled=True).astype(F32))
    hidden = activate(jnp.concatenate(both, axis=1), inv_norm)
    hidden = lax.all_gather(hidden, "dp", axis=1, tiled=True)
    part = jnp.dot(hidden, down_weight, preferred_element_type=F32).astype(BF16)
    return add(mid, lax.psum(part, "tensor"))


def body(
    residual,
    queries,
    new_keys,
    new_values,
    key_cache,
    value_cache,
    lengths,
    out_weight,
    norm_gain,
    gate_weight,
    up_weight,
    down_weight,
):
    dp = lax.axis_size("dp")
    tensor = lax.axis_size("tensor")
    steps, all_seqs, width = residual.shape
    local_seqs = queries.shape[1]
    where = jnp.stack([lax.axis_index("dp"), lax.axis_index("tensor") % 2])
    where, queries = lax.optimization_barrier((where, queries))
    heads, carried = attention_first(
        queries, new_keys, new_values, key_cache, value_cache, lengths
    )
    if dp == 4 and tensor == 4:
        weights = out_weight, gate_weight, up_weight, down_weight
        gain, heads = lax.optimization_barrier((norm_gain, heads))
        return fast(where, heads, carried, residual, gain, *weights)
    heads = jnp.stack((heads, attention_second(carried)))
    heads = heads.reshape(2, steps, local_seqs // 2, -1).swapaxes(0, 1)
    heads = heads.reshape(steps * local_seqs, -1)
    row_count = steps * all_seqs
    resid = residual.reshape(steps, dp, local_seqs, width).swapaxes(0, 1)
    weights = out_weight, norm_gain, gate_weight, up_weight, down_weight
    out = plain(gather_rows(heads, dp), resid.reshape(row_count, width), *weights, dp)
    return out.reshape(dp, steps, local_seqs, width).swapaxes(0, 1).reshape(residual.shape)


def fast(where, heads, carried, residual, gain, out_w, gate_weight, up_weight, down_weight):
    width = out_w.shape[1]
    groups = 2
    core = lambda value: lax.ppermute(value, "dp", pairs(4, 1))
    across = lambda value: lax.ppermute(value, "dp", pairs(4, 2))
    swap = lambda value: lax.ppermute(value, "tensor", pairs(4, 1))
    gain = jnp.broadcast_to(gain[None, :], (16, width))
    after = lambda value, *others: lax.optimization_barrier((value, *others))[0]

    def sum_tensor(sends, keeps, during=lambda n, held: None):
        gots = [swap(send) for send in sends]
        helds, crosses = [None, None], [None, None]
        for n in range(2):
            if n:
                gots[n] = after(gots[n], helds[0])
            keep, gots[n] = keeps(n, helds[0], gots[n])
            helds[n] = total_of(keep, gots[n])
            crosses[n] = lax.ppermute(helds[n], "tensor", pairs(4, 2))
        others = [None, None]
        for n in range(2):
            beside = during(n, helds[1 - n])
            if beside is not None:
                crosses[n] = after(crosses[n], beside)
            helds[n] = total_of(helds[n], crosses[n])
            others[n] = swap(helds[n])
            if n == 0:
                crosses[1] = after(crosses[1], helds[0])
        return helds, others

    out_w, up_w, down_w = [
        pltpu.with_memory_space_constraint(w, pltpu.VMEM) for w in (out_w, up_weight, down_weight)
    ]
    far_a = across(heads)
    heads_b = attention_second(carried)
    far_a, heads_b = lax.optimization_barrier((far_a, heads_b))
    far_b = across(heads_b)
    blocks_a = [heads, core(heads), far_a, core(far_a)]
    blocks_a, gain = lax.optimization_barrier((blocks_a, gain))
    (send_a,) = product(where, out_w, (blocks_a, 1))
    far_b, send_a = lax.optimization_barrier((far_b, send_a))
    blocks_b = [heads_b, core(heads_b), far_b, core(far_b)]
    keep_a, send_b = product(where, out_w, (blocks_a, 0), (blocks_b, 1))
    gate = []

    def keeps(n, held, got):
        if n == 0:
            return keep_a, got
        return product(where, out_w, (after(blocks_b, held), 0))[0], got

    def during(n, held):
        if n == 0:
            gate.extend(fetch(where, gate_weight, [held]))
            return gate[1]

    helds, others = sum_tensor([send_a, send_b], keeps, during)
    mid, normed, sq = middle_part(where, 0, helds, residual, gain)
    first = gate_up_first(where, normed, (gate[0], up_w))
    others, first = lax.optimization_barrier((others, first))
    mid_other, normed, sq_other = middle_part(where, 1, others, residual, gain)
    sq = total_of(sq, sq_other, dtype=F32)
    weights = gate[1], up_w
    give, keep = gate_up_second(where, normed, first, sq, weights, 1, groups)
    far = [core(x) for x in give]
    relayed = [relay(n, keep, x, sq) for n, x in enumerate(far)]
    far = [across(x) for x in relayed]
    normed, relayed = lax.optimization_barrier((normed, relayed))
    give, near = gate_up_second(where, normed, first, sq, weights, 0, groups)
    got = [core(x) for x in give]
    far[0], near, got = lax.optimization_barrier((far[0], near, got))

    def activated(n):
        mine = act(n, near, got[n], far[n], sq, width * 4)
        other = core(mine)
        return mine, across(mine), other

    def early(n):
        return down(where, down_w, (mine[n], other[n], 0, None, None))[0]

    def last(n, flip, total):
        return mine_far[n], other_far[n], 1, flip, total

    mine, mine_far, other, totals, other_far = [0] * 2, [0] * 2, [0] * 2, [0] * 2, [0] * 2
    mine[0], mine_far[0], other[0] = activated(0)
    totals[0] = early(0)
    far[1] = after(far[1], totals[0])
    mine[1], mine_far[1], other[1] = activated(1)
    mine_far[0] = after(mine_far[0], mine[1])
    other_far[0] = core(mine_far[0])
    totals[1] = early(1)
    other_far[0] = after(other_far[0], totals[1])
    (send_a,) = down(where, down_w, last(0, 1, totals[0]))
    mine_far[1] = after(mine_far[1], send_a)
    other_far[1] = core(mine_far[1])
    keep_a, send_b = down(where, down_w, last(0, 0, totals[0]), last(1, 1, totals[1]))

    def keeps(n, held, got):
        if n == 0:
            return keep_a, got
        return down(where, down_w, last(1, 0, after(totals[1], held)))[0], got

    helds, others = sum_tensor([send_a, send_b], keeps)
    outs = list(zip(helds, others))
    return final(where, [mid, mid_other], outs, residual.shape)


def solution(mesh):
    in_specs = (
        P(None, "replica", "dp"),
        P(None, ("replica", "dp"), "tensor"),
        P(None, ("replica", "dp"), "tensor", None),
        P(None, ("replica", "dp"), "tensor", None),
        P(("replica", "dp"), "tensor", None, None),
        P(("replica", "dp"), "tensor", None, None),
        P(("replica", "dp")),
        P("tensor", "dp"),
        P("dp"),
        P("dp", "tensor"),
        P("dp", "tensor"),
        P("tensor", "dp"),
    )
    out_specs = P(None, "replica", "dp")
    return jax.shard_map(body, mesh=mesh, in_specs=in_specs, out_specs=out_specs, check_vma=False)
```
